256 devices in a mesh: replica: 32 (over z, x_lo, core), tensor: 8 (over x_hi, y).
Axes of the slice: x: 4 (x_hi: 2, x_lo: 2; x = x_hi * 2 + x_lo), y: 4, z: 8, core: 2. Of those that a mesh axis runs over, the one named last changes fastest.
Arguments:
- tokens: bfloat16 [32768, 8192], P('replica', 'tensor'), may hold values from -120 to 120
- norm_gain: float32 [8192], P('tensor'), may hold values from 0.5 to 1.5
- key_weight: bfloat16 [8192, 1024], P('tensor'), may hold values from -0.0625 to 0.0625
- key_cotangent: bfloat16 [32768, 1024], P('replica', 'tensor'), may hold values from -6 to 6
- local_delta: bfloat16 [32, 320, 8192], P('replica', 'tensor'), may hold values from -12 to 12
- outer_params: float32 [320, 8192], P('tensor'), may hold values from -0.75 to 0.75
- momentum: float32 [320, 8192], P('tensor'), may hold values from -3 to 3
Outputs:
- projected_keys: bfloat16 [32768, 1024], P('replica', 'tensor')
- token_grads: bfloat16 [32768, 8192], P('replica', 'tensor')
- row_projection: float32 [32768], P('replica')
- weight_grads: bfloat16 [32, 8192, 1024], P('replica', 'tensor')
- new_params: float32 [320, 8192], P('tensor')
- new_momentum: float32 [320, 8192], P('tensor')
The draws below stay inside these ranges and needn't reach their ends.
All inputs are finite; a program needn't handle non-finite values.
Results may differ from the reference program's by a relative error of at most 0.017.
Values may be sent and summed in bfloat16 or wider, within the bound.
A program may use at most 128 MiB of HBM per device.

```python
import math
import jax
import jax.numpy as jnp
from jax import lax

D = 8192
KW = 1024
TOK_REP = 1024
WORKERS = 32
FRAG = 320
FEAT_DEV = 1024
TOKENS = 32768


def draw_tokens(key, part):
    key = jax.random.fold_in(key, 11)
    base_key, column_key, row_key = jax.random.split(key, 3)
    columns = jnp.arange(D, dtype=jnp.float32)
    ramp = jnp.exp(math.log(3.0) * columns / D)
    column_factor = jnp.exp(jax.random.uniform(column_key, (D,), jnp.float32, 0.0, math.log(3.3)))
    row_factor = jnp.exp(jax.random.uniform(row_key, (TOKENS, 1), jnp.float32, math.log(0.3), math.log(3.0)))
    base = jnp.clip(jax.random.normal(base_key, (TOKENS, D), jnp.float32), -4.0, 4.0)
    return (base * row_factor * ramp * column_factor).astype(jnp.bfloat16)


def draw_local_delta(key, part):
    key = jax.random.fold_in(key, 23)
    base_key, scale_key = jax.random.split(key, 2)
    row_scale = jnp.exp(jax.random.uniform(scale_key, (WORKERS, FRAG, 1), jnp.float32, math.log(0.01), math.log(3.0)))
    base = jnp.clip(jax.random.normal(base_key, (WORKERS, FRAG, D), jnp.float32), -4.0, 4.0)
    values = row_scale * base
    return values.astype(jnp.bfloat16)


def shard_levels(key, shape, cuts, smallest, top_value):
    level = 1.0
    for position, shards_of in cuts:
        steps = jax.random.uniform(jax.random.fold_in(jax.random.fold_in(key, 6), position), (shards_of,), jnp.float32, smallest / len(cuts), top_value / len(cuts))
        level = level * jnp.repeat(jnp.exp(steps), shape[position] // shards_of).reshape((-1,) + (1,) * (len(shape) - 1 - position))
    return level


def normal_values(stream_key, extent, spread, bound, cuts=(), kind=jnp.bfloat16):
    drawn = spread * jax.random.normal(stream_key, extent, jnp.float32)
    if cuts:
        drawn = drawn * shard_levels(stream_key, extent, cuts, -0.22, 0.18)
    return jnp.clip(drawn, -bound, bound).astype(kind)


def setup_inputs(seed: int = 0) -> dict:
    key_list = jax.random.split(jax.random.key(seed), 8)
    tokens = draw_tokens(jax.random.fold_in(key_list[7], 71), 0)
    norm_gain = jnp.clip(1.0 + 0.1 * jax.random.normal(key_list[1], (D,), jnp.float32), 0.5, 1.5)
    key_weight = normal_values(key_list[2], (D, KW), D ** -0.5, 0.0625, ((0, 8),))
    key_cotangent = normal_values(key_list[3], (TOKENS, KW), 1.0, 6.0, ((0, 32), (1, 8)))
    local_delta = draw_local_delta(jax.random.fold_in(key_list[7], 71), 0)
    outer_params = normal_values(key_list[5], (FRAG, D), 0.05, 0.75, ((0, 8),), jnp.float32)
    momentum = normal_values(key_list[6], (FRAG, D), 0.2, 3.0, ((0, 8),), jnp.float32)
    return dict(tokens=tokens, norm_gain=norm_gain, key_weight=key_weight, key_cotangent=key_cotangent, local_delta=local_delta, outer_params=outer_params, momentum=momentum)


SCALE_LOWEST = -7
SCALE_HIGHEST = 1
OUTER_RATE = 0.7
OUTER_MOMENTUM = 0.9
EPSILON = 1e-05
GRID_EDGES = ((0.25, 0.5, False), (0.75, 0.5, True), (1.25, 0.5, False), (1.75, 0.5, True), (2.5, 1.0, False), (3.5, 1.0, True), (5.0, 2.0, False))

def choose_scale(largest):
    scale_now = jnp.full(largest.shape, 2.0 ** SCALE_LOWEST, largest.dtype)
    for exponent in range(SCALE_LOWEST, SCALE_HIGHEST):
        scale_now = jnp.where(largest > 6.0 * 2.0 ** exponent, scale_now * 2.0, scale_now)
    return scale_now

def quantize_blocks(values):
    magnitude = jnp.abs(values)
    largest = lax.optimization_barrier(jnp.max(magnitude, axis=-1))
    block_scale = choose_scale(largest).astype(jnp.bfloat16)
    scale_wide = block_scale.astype(jnp.float32)[..., None]
    levels = jnp.zeros_like(magnitude)
    for edge_value, step_size, upward in GRID_EDGES:
        threshold = edge_value * scale_wide
        passed = magnitude >= threshold if upward else magnitude > threshold
        levels = levels + jnp.where(passed, step_size, 0.0).astype(levels.dtype)
    block_code = jnp.where(values < 0, -levels, levels).astype(jnp.bfloat16)
    return (block_code, block_scale)

def expand_blocks(block_code, block_scale):
    return block_code.astype(jnp.float32) * block_scale.astype(jnp.float32)[..., None]

def reference(tokens, norm_gain, key_weight, key_cotangent, local_delta, outer_params, momentum):

    def replica_step(replica_pair):
        rows_in, cotangent = replica_pair
        tok_float = rows_in.astype(jnp.float32)
        mean_square = lax.optimization_barrier(jnp.sum(tok_float * tok_float, axis=1, keepdims=True)) / D
        inv_rms = lax.rsqrt(mean_square + EPSILON)
        unit_rows = tok_float * inv_rms
        normed = (unit_rows * norm_gain).astype(jnp.bfloat16)
        block_rows = normed.reshape(TOK_REP, D // FEAT_DEV, FEAT_DEV).astype(jnp.float32)
        block_weight = key_weight.reshape(D // FEAT_DEV, FEAT_DEV, KW).astype(jnp.float32)
        key_parts = jnp.einsum('tbf,bfk->btk', block_rows, block_weight).astype(jnp.bfloat16)
        key_out = lax.optimization_barrier(jnp.sum(key_parts.astype(jnp.float32), axis=0)).astype(jnp.bfloat16)
        grad_rows = jnp.dot(normed.T, cotangent, preferred_element_type=jnp.float32).astype(jnp.bfloat16)
        d_normed = jnp.dot(cotangent, key_weight.T, preferred_element_type=jnp.float32)
        d_scaled = d_normed * norm_gain
        projected = lax.optimization_barrier(jnp.sum(d_scaled * unit_rows, axis=1, keepdims=True)) / D
        grad_tokens = (inv_rms * (d_scaled - unit_rows * projected)).astype(jnp.bfloat16)
        row_out = projected[:, 0] * jnp.sqrt(jnp.float32(D))
        return (key_out, grad_tokens, grad_rows, row_out)
    key_out, grad_tokens, weight_grads, row_out = lax.map(replica_step, (tokens.reshape(WORKERS, TOK_REP, D), key_cotangent.reshape(WORKERS, TOK_REP, KW)))
    projected_keys = key_out.reshape(TOKENS, KW)
    token_grads = grad_tokens.reshape(TOKENS, D)
    row_projection = row_out.reshape(TOKENS)

    def add_worker(running_total, worker_delta):
        block_code, block_scale = quantize_blocks(worker_delta.astype(jnp.float32).reshape(FRAG, D // 32, 32))
        return (running_total + expand_blocks(block_code, block_scale), None)
    running_total = lax.scan(add_worker, jnp.zeros((FRAG, D // 32, 32), jnp.float32), local_delta)[0]
    average = running_total / WORKERS
    average_codes, average_scales = quantize_blocks(average)
    update = expand_blocks(average_codes, average_scales).reshape(FRAG, D)
    new_momentum = OUTER_MOMENTUM * momentum + update
    new_params = outer_params - OUTER_RATE * (update + OUTER_MOMENTUM * new_momentum)
    return (projected_keys, token_grads, row_projection, weight_grads, new_params, new_momentum)
```

```python
import functools
import math

import jax
import jax.numpy as jnp
from jax import lax
from jax.experimental import pallas as pl
from jax.experimental.pallas import tpu as pltpu
from jax.sharding import PartitionSpec as P

SCALE_LOWEST = -7
SCALE_HIGHEST = 1
OUTER_RATE = 0.7
OUTER_MOMENTUM = 0.9
EPSILON = 1e-05
GRID_EDGES = (
    (0.25, 0.5, False),
    (0.75, 0.5, True),
    (1.25, 0.5, False),
    (1.75, 0.5, True),
    (2.5, 1.0, False),
    (3.5, 1.0, True),
    (5.0, 2.0, False),
)
MESH = pl.DeviceIdType.MESH
LANES = 128
NX, NY = 4, 4
GROUP = 8
LOCAL = 4
N_REMOTE = 80
N_LOCAL = 16
F32 = jnp.float32
BF16 = jnp.bfloat16


def quantized(values, ones_blocks):
    magnitude = jnp.abs(values)
    weight = jnp.full(values.shape, 1.0, F32)
    for exponent in range(SCALE_LOWEST, SCALE_HIGHEST):
        weight = jnp.where(
            magnitude > 6.0 * 2.0**exponent, 64.0 ** (exponent - SCALE_LOWEST + 1), weight
        )
    total = jnp.dot(weight.astype(BF16), ones_blocks, preferred_element_type=F32)
    scale = jnp.full(values.shape, 2.0**SCALE_LOWEST, F32)
    back = jnp.full(values.shape, 2.0**-SCALE_LOWEST, F32)
    for exponent in range(SCALE_LOWEST, SCALE_HIGHEST):
        above = total >= 64.0 ** (exponent - SCALE_LOWEST + 1)
        scale = jnp.where(above, 2.0 ** (exponent + 1), scale)
        back = jnp.where(above, 2.0 ** -(exponent + 1), back)
    ratio = magnitude * back
    level = jnp.zeros(values.shape, F32)
    reached = 0.0
    for edge, step, upward in GRID_EDGES:
        reached += step
        passed = ratio >= edge if upward else ratio > edge
        level = jnp.where(passed, reached, level)
    level = level * scale
    return jnp.where(values < 0, -level, level)


def block_ones():
    row = lax.broadcasted_iota(jnp.int32, (LANES, LANES), 0) // 32
    column = lax.broadcasted_iota(jnp.int32, (LANES, LANES), 1) // 32
    return jnp.where(row == column, 1.0, 0.0).astype(BF16)


def kernel(
    full_width,
    tok_hbm,
    gain_ref,
    weight_hbm,
    cot_hbm,
    delta_ref,
    keys_hbm,
    tgrad_hbm,
    rowproj_ref,
    wgrad_hbm,
    update_ref,
    tok,
    wt,
    normed,
    normed_t,
    parts,
    cotg,
    dscaled,
    wgrad,
    tgrad,
    keys_out,
    inv_col,
    inv_row,
    other_row,
    sums,
    projs,
    x_relay,
    merge_in,
    merge_out,
    near,
    far_send,
    far_relay,
    far_in,
    qsend,
    r1,
    s1,
    r2,
    upd,
    ssem,
    rsem,
    lsem,
):
    r = lax.axis_index("replica")
    t = lax.axis_index("tensor")
    zs = lax.axis_size("replica") // LOCAL
    core = r % 2
    x_lo = (r // 2) % 2
    c = r % LOCAL
    z = r // LOCAL
    x_hi = t // NY
    y = t % NY
    x = x_hi * 2 + x_lo
    tokens_n, feats = tok.shape
    half = tokens_n // 2
    H = (pl.ds(0, half), pl.ds(half, half))
    yp, ym, y2 = (y + 1) % NY, (y + 3) % NY, (y + 2) % NY
    xp, xm = (x + 1) % NX, (x + 3) % NX

    def at_x(x_new):
        return ((z * 2 + x_new % 2) * 2 + core, (x_new // 2) * NY + y)

    dev_yp = (r, x_hi * NY + yp)
    dev_ym = (r, x_hi * NY + ym)
    dev_xp, dev_xm = at_x(xp), at_x(xm)
    dev_xlo = (z * LOCAL + (c + 2) % LOCAL, t)
    dev_core = (z * LOCAL + x_lo * 2 + (1 - core), t)
    c_xlo = (c + 2) % LOCAL
    c_core = x_lo * 2 + (1 - core)
    c_diag = (1 - x_lo) * 2 + (1 - core)
    t_far = (1 - x_hi) * NY + y

    names = {}
    pending = []

    def index_of(name):
        return names.setdefault(name, len(names))

    def send(name, src, dst, device):
        i = index_of(name)
        copy = pltpu.make_async_remote_copy(
            src_ref=src,
            dst_ref=dst,
            send_sem=ssem.at[i],
            recv_sem=rsem.at[i],
            device_id=device,
            device_id_type=MESH,
        )
        copy.start()
        pending.append(copy)

    def arrive(name, landing):
        i = index_of(name)
        pltpu.make_async_remote_copy(
            src_ref=landing,
            dst_ref=landing,
            send_sem=ssem.at[i],
            recv_sem=rsem.at[i],
            device_id=dev_yp,
            device_id_type=MESH,
        ).wait_recv()

    local = {}

    def fetch(name, src, dst):
        i = len(local)
        copy = pltpu.make_async_copy(src, dst, lsem.at[i])
        copy.start()
        local[name] = copy

    for h in range(2):
        fetch(("tok", h), tok_hbm.at[H[h]], tok.at[H[h]])
    fetch("weight", weight_hbm, wt)
    fetch("cot", cot_hbm, cotg.at[t])

    barrier = pltpu.get_barrier_semaphore()
    partners = [(r, (t + d) % GROUP) for d in range(1, GROUP)]
    partners += [(((z + d) % zs) * LOCAL + c, t) for d in range(1, zs)]
    partners += [dev_xp, dev_xm, dev_core, (z * LOCAL + c_diag, t)]
    for device in partners:
        pl.semaphore_signal(barrier, inc=1, device_id=device, device_id_type=MESH)
    pl.semaphore_wait(barrier, len(partners))

    send("x0", cot_hbm.at[H[0]], x_relay.at[0], dev_xp)
    send("x1", cot_hbm.at[H[1]], x_relay.at[1], dev_xm)
    send("own_p0", cot_hbm.at[H[0]], cotg.at[t, H[0]], dev_yp)
    send("own_m1", cot_hbm.at[H[1]], cotg.at[t, H[1]], dev_ym)
    send("own_p1", cot_hbm.at[H[1]], cotg.at[t, H[1]], dev_yp)
    send("own_m0", cot_hbm.at[H[0]], cotg.at[t, H[0]], dev_ym)

    blocks = tokens_n // LANES
    fblocks = feats // LANES

    def lane_sum_row(acc):
        return jnp.sum(acc.T, axis=0, keepdims=True)

    def column_of(row):
        return jnp.broadcast_to(row, (LANES, LANES)).T

    def sum_squares():
        @pl.loop(0, blocks // 2)
        def _(b):
            one(b)

        local[("tok", 1)].wait()

        @pl.loop(blocks // 2, blocks)
        def _(b):
            one(b)

    def one(b):
        rows = pl.ds(pl.multiple_of(b * LANES, LANES), LANES)
        acc = jnp.zeros((LANES, LANES), F32)
        for j in range(fblocks):
            v = tok[rows, j * LANES : (j + 1) * LANES].astype(F32)
            acc = acc + v * v
        sums[t, pl.ds(b, 1), :] = lane_sum_row(acc)

    local[("tok", 0)].wait()
    sum_squares()
    for d in range(1, GROUP):
        send(("sum", d), sums.at[t], sums.at[t], (r, (t + d) % GROUP))

    def relay_x():
        arrive("x0", x_relay.at[0])
        send("xf0", x_relay.at[0], cotg.at[(xm // 2) * NY + y, H[0]], dev_xp)
        arrive("x1", x_relay.at[1])
        send("xf1", x_relay.at[1], cotg.at[(xp // 2) * NY + y, H[1]], dev_xm)

    relay_x()

    share = delta_ref.shape[1] // (LOCAL * zs)
    frag = delta_ref.shape[0]
    width = share // LANES

    def quantize_share(s):
        ones_blocks = block_ones()
        pieces = [
            delta_ref[:, pl.ds(pl.multiple_of(s * share + k * LANES, LANES), LANES)].astype(F32)
            for k in range(width)
        ]
        values = jnp.concatenate(pieces, axis=0)
        qsend[s // zs, s % zs] = quantized(values, ones_blocks).astype(BF16)

    @pl.loop(0, LOCAL * zs)
    def _(s):
        quantize_share(s)

    for d in range(1, LOCAL):
        to = (c + d) % LOCAL
        send(("r1", d), qsend.at[to], r1.at[c], (z * LOCAL + to, t))

    t_ym, t_yp, t_y2 = x_hi * NY + ym, x_hi * NY + yp, x_hi * NY + y2
    f_ym, f_yp, f_y2 = ((1 - x_hi) * NY + k for k in (ym, yp, y2))
    arrive("own_p0", cotg.at[t_ym, H[0]])
    send("own_pp", cotg.at[t_ym, H[0]], cotg.at[t_ym, H[0]], dev_yp)
    arrive("own_m1", cotg.at[t_yp, H[1]])
    send("own_mm", cotg.at[t_yp, H[1]], cotg.at[t_yp, H[1]], dev_ym)

    for d in range(1, GROUP):
        arrive(("sum", d), sums.at[(t + GROUP - d) % GROUP])
    total = sums[0]
    for k in range(1, GROUP):
        total = total + sums[k]
    inv_row[...] = lax.rsqrt(total / full_width + EPSILON)

    @pl.loop(0, blocks)
    def _(b):
        rows = pl.ds(pl.multiple_of(b * LANES, LANES), LANES)
        column = column_of(inv_row[pl.ds(b, 1), :])
        inv_col[rows, :] = column
        for j in range(fblocks):
            cols = slice(j * LANES, (j + 1) * LANES)
            value = (tok[rows, cols].astype(F32) * column * gain_ref[:, cols]).astype(BF16)
            normed[rows, cols] = value
            normed_t[cols, rows] = value.T

    arrive("xf0", cotg.at[t_far, H[0]])
    send("far_p0", cotg.at[t_far, H[0]], cotg.at[t_far, H[0]], dev_yp)
    send("far_m0", cotg.at[t_far, H[0]], cotg.at[t_far, H[0]], dev_ym)
    arrive("xf1", cotg.at[t_far, H[1]])
    send("far_m1", cotg.at[t_far, H[1]], cotg.at[t_far, H[1]], dev_ym)
    send("far_p1", cotg.at[t_far, H[1]], cotg.at[t_far, H[1]], dev_yp)

    local["weight"].wait()

    @pl.loop(0, GROUP // 2)
    def _(n):
        cols = pl.ds(pl.multiple_of(n * 2 * LANES, LANES), 2 * LANES)
        for h in range(2):
            part = jnp.dot(normed[H[h], :], wt[:, cols], preferred_element_type=F32)
            parts[2 * n, H[h]] = part[:, :LANES].astype(BF16)
            parts[2 * n + 1, H[h]] = part[:, LANES:].astype(BF16)

    def target(s, y_new):
        return ((1 - x_hi) if s == 0 else x_hi) * NY + y_new

    for s in range(2):
        send(("d2p", s), parts.at[target(s, y2), H[0]], merge_in.at[s, 0], dev_yp)
        send(("d2m", s), parts.at[target(s, y2), H[1]], merge_in.at[s, 1], dev_ym)
        send(("d1p", s), parts.at[target(s, yp), H[1]], near.at[s, 0, H[1]], dev_yp)
        send(("d1m", s), parts.at[target(s, ym), H[0]], near.at[s, 1, H[0]], dev_ym)

    for d in range(1, LOCAL):
        arrive(("r1", d), r1.at[(c + LOCAL - d) % LOCAL])
    r1[c] = qsend[c]

    @pl.loop(0, zs)
    def _(k):
        s1[k] = (r1[0, k].astype(F32) + r1[1, k].astype(F32)) + (
            r1[2, k].astype(F32) + r1[3, k].astype(F32)
        )

    for d in range(1, zs):
        to = (z + d) % zs
        send(("r2", d), s1.at[to], r2.at[z], (to * LOCAL + c, t))
    r2[z] = s1[z]

    arrive("far_p0", cotg.at[f_ym, H[0]])
    send("far_pp", cotg.at[f_ym, H[0]], cotg.at[f_ym, H[0]], dev_yp)
    arrive("far_m1", cotg.at[f_yp, H[1]])
    send("far_mm", cotg.at[f_yp, H[1]], cotg.at[f_yp, H[1]], dev_ym)

    def weight_grad_pair(p):
        rhs = jnp.concatenate([cotg[2 * p], cotg[2 * p + 1]], axis=1)
        cols = pl.ds(pl.multiple_of(p * 2 * LANES, LANES), 2 * LANES)
        for h in range(2):
            rows = slice(h * (feats // 2), (h + 1) * (feats // 2))
            wgrad[rows, cols] = jnp.dot(
                normed_t[rows, :], rhs, preferred_element_type=F32
            ).astype(BF16)

    def weight_grad_side(x_side):
        @pl.loop(0, 2)
        def _(k):
            weight_grad_pair(x_side * 2 + k)

    local["cot"].wait()
    arrive("own_p1", cotg.at[t_ym, H[1]])
    arrive("own_m0", cotg.at[t_yp, H[0]])
    arrive("own_pp", cotg.at[t_y2, H[0]])
    arrive("own_mm", cotg.at[t_y2, H[1]])
    weight_grad_side(x_hi)

    def merge(s):
        arrive(("d2p", s), merge_in.at[s, 0])
        merge_out[s, 0] = (
            merge_in[s, 0].astype(F32) + parts[target(s, yp), H[0]].astype(F32)
        ).astype(BF16)
        send(("d1pp", s), merge_out.at[s, 0], near.at[s, 0, H[0]], dev_yp)
        arrive(("d2m", s), merge_in.at[s, 1])
        merge_out[s, 1] = (
            merge_in[s, 1].astype(F32) + parts[target(s, ym), H[1]].astype(F32)
        ).astype(BF16)
        send(("d1mm", s), merge_out.at[s, 1], near.at[s, 1, H[1]], dev_ym)

    merge(0)

    for d in range(1, zs):
        arrive(("r2", d), r2.at[(z + zs - d) % zs])
    total = r2[0]
    for k in range(1, zs):
        total = total + r2[k]
    upd[c, z] = quantized(total / (LOCAL * zs), block_ones()).astype(BF16)
    for d in range(1, zs):
        send(("r3", d), upd.at[c, z], upd.at[c, z], (((z + d) % zs) * LOCAL + c, t))

    merge(1)

    arrive("far_m0", cotg.at[f_yp, H[0]])
    arrive("far_p1", cotg.at[f_ym, H[1]])
    arrive("far_pp", cotg.at[f_y2, H[0]])
    arrive("far_mm", cotg.at[f_y2, H[1]])
    weight_grad_side(1 - x_hi)
    fetch("wgrad", wgrad, wgrad_hbm)

    for d in range(1, zs):
        arrive(("r3", d), upd.at[c, (z + zs - d) % zs])
    send("r4x", upd.at[c], upd.at[c], dev_xlo)
    send("r4c", upd.at[c], upd.at[c], dev_core)

    step = 2 * LANES if tokens_n % (2 * LANES) == 0 else LANES

    @pl.loop(0, tokens_n // step)
    def _(m):
        rows = pl.ds(pl.multiple_of(m * step, step), step)
        lhs = jnp.concatenate([cotg[k, rows, :] for k in range(GROUP)], axis=1)
        d = lax.dot_general(lhs, wt[...], (((1,), (1,)), ((), ())), preferred_element_type=F32)
        d = d * gain_ref[...]
        dscaled[rows, :] = d
        acc = jnp.zeros((step, LANES), F32)
        for j in range(fblocks):
            cols = slice(j * LANES, (j + 1) * LANES)
            acc = acc + d[:, cols] * tok[rows, cols].astype(F32)
        for k in range(step // LANES):
            projs[t, pl.ds(m * (step // LANES) + k, 1), :] = lane_sum_row(
                acc[k * LANES : (k + 1) * LANES]
            )

    for d in range(1, GROUP):
        send(("proj", d), projs.at[t], projs.at[t], (r, (t + d) % GROUP))

    def near_sum(s, h):
        own = parts[target(s, y), H[h]].astype(F32)
        return own + (near[s, 0, H[h]].astype(F32) + near[s, 1, H[h]].astype(F32))

    def near_arrive(s):
        arrive(("d1p", s), near.at[s, 0, H[1]])
        arrive(("d1m", s), near.at[s, 1, H[0]])
        arrive(("d1pp", s), near.at[s, 0, H[0]])
        arrive(("d1mm", s), near.at[s, 1, H[1]])

    near_arrive(0)
    far_send[H[0], :] = near_sum(0, 0).astype(BF16)
    send("k0", far_send.at[H[0]], far_relay.at[0], dev_xp)
    far_send[H[1], :] = near_sum(0, 1).astype(BF16)
    send("k1", far_send.at[H[1]], far_relay.at[1], dev_xm)

    arrive("r4x", upd.at[c_xlo])
    send("r4xc", upd.at[c_xlo], upd.at[c_xlo], dev_core)

    arrive("k0", far_relay.at[0])
    send("kf0", far_relay.at[0], far_in.at[H[0]], dev_xp)
    arrive("k1", far_relay.at[1])
    send("kf1", far_relay.at[1], far_in.at[H[1]], dev_xm)

    for d in range(1, GROUP):
        arrive(("proj", d), projs.at[(t + GROUP - d) % GROUP])
    total = projs[0]
    for k in range(1, GROUP):
        total = total + projs[k]
    projected = total * inv_row[...] / full_width
    rowproj_ref[...] = projected * math.sqrt(full_width)
    other_row[...] = projected * inv_row[...] * inv_row[...]

    @pl.loop(0, blocks)
    def _(b):
        rows = pl.ds(pl.multiple_of(b * LANES, LANES), LANES)
        column = inv_col[rows, :]
        other = column_of(other_row[pl.ds(b, 1), :])
        for j in range(fblocks):
            cols = slice(j * LANES, (j + 1) * LANES)
            tgrad[rows, cols] = (
                column * dscaled[rows, cols] - tok[rows, cols].astype(F32) * other
            ).astype(BF16)

    fetch("tgrad", tgrad, tgrad_hbm)

    arrive("r4c", upd.at[c_core])
    arrive("r4xc", upd.at[c_diag])

    @pl.loop(0, LOCAL * zs)
    def _(s):
        value = upd[s // zs, s % zs].astype(F32)
        for k in range(width):
            cols = pl.ds(pl.multiple_of(s * share + k * LANES, LANES), LANES)
            update_ref[:, cols] = value[k * frag : (k + 1) * frag, :]

    near_arrive(1)
    arrive("kf0", far_in.at[H[0]])
    keys_out[H[0], :] = (near_sum(1, 0) + far_in[H[0], :].astype(F32)).astype(BF16)
    arrive("kf1", far_in.at[H[1]])
    keys_out[H[1], :] = (near_sum(1, 1) + far_in[H[1], :].astype(F32)).astype(BF16)
    fetch("keys", keys_out, keys_hbm)

    for copy in pending:
        copy.wait_send()
    for name in ("wgrad", "tgrad", "keys"):
        local[name].wait()


def per_device(tokens, norm_gain, key_weight, key_cotangent, local_delta, outer_params, momentum):
    tok_n, feats = tokens.shape
    heads = key_weight.shape[1]
    full_width = feats * lax.axis_size("tensor")
    workers = lax.axis_size("replica")
    zs = workers // LOCAL
    frag, row_width = outer_params.shape
    share_rows = frag * row_width // workers // LANES
    half = tok_n // 2
    kb = key_cotangent.shape[1]
    any_spec = pl.BlockSpec(memory_space=pl.ANY)
    vmem = pl.BlockSpec(memory_space=pltpu.VMEM)
    blocks = tok_n // LANES
    keys, tgrad, rowproj, wgrad, update = pl.pallas_call(
        functools.partial(kernel, full_width),
        out_shape=(
            jax.ShapeDtypeStruct((tok_n, kb), BF16),
            jax.ShapeDtypeStruct((tok_n, feats), BF16),
            jax.ShapeDtypeStruct((blocks, LANES), F32),
            jax.ShapeDtypeStruct((feats, heads), BF16),
            jax.ShapeDtypeStruct((frag, row_width), F32),
        ),
        in_specs=[any_spec, vmem, any_spec, any_spec, vmem],
        out_specs=(any_spec, any_spec, vmem, any_spec, vmem),
        scratch_shapes=[
            pltpu.VMEM((tok_n, feats), BF16),
            pltpu.VMEM((feats, heads), BF16),
            pltpu.VMEM((tok_n, feats), BF16),
            pltpu.VMEM((feats, tok_n), BF16),
            pltpu.VMEM((GROUP, tok_n, kb), BF16),
            pltpu.VMEM((GROUP, tok_n, kb), BF16),
            pltpu.VMEM((tok_n, feats), F32),
            pltpu.VMEM((feats, heads), BF16),
            pltpu.VMEM((tok_n, feats), BF16),
            pltpu.VMEM((tok_n, kb), BF16),
            pltpu.VMEM((tok_n, LANES), F32),
            pltpu.VMEM((blocks, LANES), F32),
            pltpu.VMEM((blocks, LANES), F32),
            pltpu.VMEM((GROUP, blocks, LANES), F32),
            pltpu.VMEM((GROUP, blocks, LANES), F32),
            pltpu.VMEM((2, half, kb), BF16),
            pltpu.VMEM((2, 2, half, kb), BF16),
            pltpu.VMEM((2, 2, half, kb), BF16),
            pltpu.VMEM((2, 2, tok_n, kb), BF16),
            pltpu.VMEM((tok_n, kb), BF16),
            pltpu.VMEM((2, half, kb), BF16),
            pltpu.VMEM((tok_n, kb), BF16),
            pltpu.VMEM((LOCAL, zs, share_rows, LANES), BF16),
            pltpu.VMEM((LOCAL, zs, share_rows, LANES), BF16),
            pltpu.VMEM((zs, share_rows, LANES), F32),
            pltpu.VMEM((zs, share_rows, LANES), F32),
            pltpu.VMEM((LOCAL, zs, share_rows, LANES), BF16),
            pltpu.SemaphoreType.DMA((N_REMOTE,)),
            pltpu.SemaphoreType.DMA((N_REMOTE,)),
            pltpu.SemaphoreType.DMA((N_LOCAL,)),
        ],
        compiler_params=pltpu.CompilerParams(
            collective_id=0, has_side_effects=True, vmem_limit_bytes=44 * 1024 * 1024
        ),
        cost_estimate=pl.CostEstimate(
            flops=6 * tok_n * feats * heads, bytes_accessed=16 * 1024 * 1024, transcendentals=0
        ),
    )(tokens, norm_gain.reshape(1, feats), key_weight, key_cotangent, local_delta[0])
    new_momentum = OUTER_MOMENTUM * momentum + update
    new_params = outer_params - OUTER_RATE * (update + OUTER_MOMENTUM * new_momentum)
    return (keys, tgrad, rowproj.reshape(tok_n), wgrad[None], new_params, new_momentum)


def solution(mesh):
    placed = (
        P("replica", "tensor"),
        P("tensor"),
        P("tensor", None),
        P("replica", "tensor"),
        P("replica", "tensor", None),
        P("tensor", None),
        P("tensor", None),
    )
    return jax.shard_map(
        per_device,
        mesh=mesh,
        in_specs=placed,
        out_specs=(
            P("replica", "tensor"),
            P("replica", "tensor"),
            P("replica"),
            P("replica", "tensor", None),
            P("tensor", None),
            P("tensor", None),
        ),
        check_vma=False,
    )
```

```python
import functools
import math

import jax
import jax.numpy as jnp
from jax import lax
from jax.experimental import pallas as pl
from jax.experimental.pallas import tpu as pltpu
from jax.sharding import PartitionSpec as P

SCALE_LOWEST = -7
SCALE_HIGHEST = 1
OUTER_RATE = 0.7
OUTER_MOMENTUM = 0.9
EPSILON = 1e-05
GRID_EDGES = (
    (0.25, 0.5, False),
    (0.75, 0.5, True),
    (1.25, 0.5, False),
    (1.75, 0.5, True),
    (2.5, 1.0, False),
    (3.5, 1.0, True),
    (5.0, 2.0, False),
)
MESH = pl.DeviceIdType.MESH
LANES = 128
NY = 4
GROUP = 8
LOCAL = 4
N_REMOTE = 96
N_LOCAL = 16
F32 = jnp.float32
BF16 = jnp.bfloat16


def quantized(values, ones_blocks):
    kind = values.dtype
    magnitude = jnp.abs(values)

    def const(value):
        return jnp.full(values.shape, value, kind)

    weight = const(1.0)
    for exponent in range(SCALE_LOWEST, SCALE_HIGHEST):
        weight = jnp.where(
            magnitude > const(6.0 * 2.0**exponent),
            const(64.0 ** (exponent - SCALE_LOWEST + 1)),
            weight,
        )
    total = jnp.dot(weight.astype(BF16), ones_blocks, preferred_element_type=F32).astype(kind)
    scale = const(2.0**SCALE_LOWEST)
    back = const(2.0**-SCALE_LOWEST)
    for exponent in range(SCALE_LOWEST, SCALE_HIGHEST):
        above = total >= const(64.0 ** (exponent - SCALE_LOWEST + 1))
        scale = jnp.where(above, const(2.0 ** (exponent + 1)), scale)
        back = jnp.where(above, const(2.0 ** -(exponent + 1)), back)
    ratio = magnitude * back
    level = const(0.0)
    reached = 0.0
    for edge, step, upward in GRID_EDGES:
        reached += step
        passed = ratio >= const(edge) if upward else ratio > const(edge)
        level = jnp.where(passed, const(reached), level)
    level = level * scale
    return jnp.where(values < const(0.0), -level, level)


def block_ones():
    row = lax.broadcasted_iota(jnp.int32, (LANES, LANES), 0) // 32
    column = lax.broadcasted_iota(jnp.int32, (LANES, LANES), 1) // 32
    return jnp.where(row == column, 1.0, 0.0).astype(BF16)


def kernel(
    full_width,
    tok_hbm,
    gain_hbm,
    weight_hbm,
    cot_hbm,
    delta_hbm,
    keys_ref,
    tgrad_ref,
    rowproj_ref,
    wgrad_ref,
    update_ref,
    tok,
    gain,
    delta,
    wt,
    scaled,
    normed_t,
    parts,
    cotg,
    dscaled,
    inv_col,
    inv_row,
    other_row,
    sums,
    projs,
    gin,
    xout,
    cin,
    two_out,
    merge_in,
    merge_out,
    near,
    qsend,
    r1,
    s1,
    r2,
    upd,
    ready,
    ssem,
    rsem,
    lsem,
):
    r = lax.axis_index("replica")
    t = lax.axis_index("tensor")
    zs = lax.axis_size("replica") // LOCAL
    core = r % 2
    x_lo = (r // 2) % 2
    z = r // LOCAL
    x_hi = t // NY
    y = t % NY
    tokens_n, feats = tok.shape
    half = tokens_n // 2
    H = (pl.ds(0, half), pl.ds(half, half))
    yp, ym, y2 = (y + 1) % NY, (y + 3) % NY, (y + 2) % NY
    e = core * 2 + x_lo
    e_xlo = core * 2 + (1 - x_lo)
    e_core = (1 - core) * 2 + x_lo
    e_diag = (1 - core) * 2 + (1 - x_lo)

    def of_local(z_new, e_new):
        return ((z_new * 2 + e_new % 2) * 2 + e_new // 2, t)

    dev_yp = (r, x_hi * NY + yp)
    dev_ym = (r, x_hi * NY + ym)
    ways = (dev_yp, dev_ym)
    t_far = (1 - x_hi) * NY + y
    dev_far = (r, t_far)

    names = {}
    pending = []

    def index_of(name):
        return names.setdefault(name, len(names))

    def send(name, src, dst, device):
        i = index_of(name)
        copy = pltpu.make_async_remote_copy(
            src_ref=src,
            dst_ref=dst,
            send_sem=ssem.at[i],
            recv_sem=rsem.at[i],
            device_id=device,
            device_id_type=MESH,
        )
        copy.start()
        pending.append(copy)

    def arrive(name, landing):
        i = index_of(name)
        pltpu.make_async_remote_copy(
            src_ref=landing,
            dst_ref=landing,
            send_sem=ssem.at[i],
            recv_sem=rsem.at[i],
            device_id=dev_yp,
            device_id_type=MESH,
        ).wait_recv()

    local = {}

    def fetch(name, src, dst):
        i = len(local)
        copy = pltpu.make_async_copy(src, dst, lsem.at[i])
        copy.start()
        local[name] = copy

    blocks = tokens_n // LANES
    fblocks = feats // LANES
    share = delta.shape[1] // (LOCAL * zs)
    frag = delta.shape[0]
    width = share // LANES
    t_ym, t_yp, t_y2 = x_hi * NY + ym, x_hi * NY + yp, x_hi * NY + y2
    f_ym, f_yp, f_y2 = ((1 - x_hi) * NY + k for k in (ym, yp, y2))

    def rows_of(b):
        return pl.ds(pl.multiple_of(b * LANES, LANES), LANES)

    def lane_sum_row(acc):
        return jnp.sum(acc.T, axis=0, keepdims=True)

    def column_of(row):
        return jnp.broadcast_to(row, (LANES, LANES)).T

    def load():
        fetch("delta", delta_hbm, delta)
        fetch("gain", gain_hbm, gain)
        for h in range(2):
            fetch(("tok", h), tok_hbm.at[H[h]], tok.at[H[h]])
        fetch("weight", weight_hbm, wt)
        fetch("cot", cot_hbm, cotg.at[t])

    def greet():
        barrier = pltpu.get_barrier_semaphore()

        def tell(device):
            pl.semaphore_signal(barrier, inc=1, device_id=device, device_id_type=MESH)

        for d in range(1, GROUP):
            tell((r - core, (t + d) % GROUP))
        tell(of_local(z, 1 - x_lo))

        @pl.when(core == 1)
        def _():
            tell(of_local(z, x_lo))

        for d in range(1, zs):
            tell(of_local((z + d) % zs, 2 + x_lo))

    def collect(collector, count, ready_sem):
        @pl.when(core == collector)
        def _():
            pl.semaphore_wait(pltpu.get_barrier_semaphore(), count)
            pl.semaphore_signal(
                ready_sem, inc=1, device_id=of_local(z, e_core), device_id_type=MESH
            )

        @pl.when(core != collector)
        def _():
            pl.semaphore_wait(ready_sem, 1)

    def meet():
        collect(0, 2 * GROUP + 1, ready.at[0])

    def meet_z():
        collect(1, 2 * (zs - 1), ready.at[1])

    def cot_start(i):
        h, k = H[i], H[1 - i]
        send(("own_p", i), cot_hbm.at[h], cotg.at[t, h], dev_yp)
        send(("own_m", 1 - i), cot_hbm.at[k], cotg.at[t, k], dev_ym)
        send(("c", i), cot_hbm.at[h], cotg.at[t, h], dev_far)

    def cot_onward(way):
        block = (t_ym, t_yp)[way]
        arrive((("own_p", "own_m")[way], way), cotg.at[block, H[way]])
        send(("own_on", way), cotg.at[block, H[way]], cotg.at[block, H[way]], ways[way])

    def cot_far_start(h):
        arrive(("c", h), cotg.at[t_far, H[h]])
        send(("far_p", h), cotg.at[t_far, H[h]], cotg.at[t_far, H[h]], dev_yp)
        send(("far_m", h), cotg.at[t_far, H[h]], cotg.at[t_far, H[h]], dev_ym)

    def cot_far_onward(way):
        block = (f_ym, f_yp)[way]
        arrive((("far_p", "far_m")[way], way), cotg.at[block, H[way]])
        send(("far_on", way), cotg.at[block, H[way]], cotg.at[block, H[way]], ways[way])

    def cot_own_end():
        local["cot"].wait()
        arrive(("own_p", 1), cotg.at[t_ym, H[1]])
        arrive(("own_m", 0), cotg.at[t_yp, H[0]])
        arrive(("own_on", 0), cotg.at[t_y2, H[0]])
        arrive(("own_on", 1), cotg.at[t_y2, H[1]])

    def cot_far_end():
        arrive(("far_m", 0), cotg.at[f_yp, H[0]])
        arrive(("far_p", 1), cotg.at[f_ym, H[1]])
        arrive(("far_on", 0), cotg.at[f_y2, H[0]])
        arrive(("far_on", 1), cotg.at[f_y2, H[1]])

    def sum_squares():
        def one(b):
            rows = rows_of(b)
            acc = jnp.zeros((LANES, LANES), F32)
            for j in range(fblocks):
                cols = slice(j * LANES, (j + 1) * LANES)
                v = tok[rows, cols].astype(F32)
                acc = acc + v * v
                scaled[rows, cols] = (v * gain[:, cols]).astype(BF16)
            sums[t, pl.ds(b, 1), :] = lane_sum_row(acc)

        local["gain"].wait()
        for h in range(2):
            local[("tok", h)].wait()
            pl.loop(h * blocks // 2, (h + 1) * blocks // 2)(one)

    def sum_squares_send():
        for d in range(1, GROUP):
            send(("sum", d), sums.at[t], sums.at[t], (r, (t + d) % GROUP))

    def sum_squares_end():
        for d in range(1, GROUP):
            arrive(("sum", d), sums.at[(t + GROUP - d) % GROUP])
        total = sums[0]
        for k in range(1, GROUP):
            total = total + sums[k]
        inv_row[...] = lax.rsqrt(total / full_width + EPSILON)

    def normed_rows():
        @pl.loop(0, blocks)
        def _(b):
            rows = rows_of(b)
            column = column_of(inv_row[pl.ds(b, 1), :])
            inv_col[rows, :] = column
            for j in range(fblocks):
                cols = slice(j * LANES, (j + 1) * LANES)
                value = (tok[rows, cols].astype(F32) * column * gain[:, cols]).astype(BF16)
                normed_t[cols, rows] = value.T

    def weight_ready():
        local["weight"].wait()

    def key_parts(x_side):
        @pl.loop(0, 2)
        def _(k):
            n = x_side * 2 + k
            cols = pl.ds(pl.multiple_of(n * 2 * LANES, LANES), 2 * LANES)
            for h in range(2):
                part = jnp.dot(scaled[H[h], :], wt[:, cols], preferred_element_type=F32)
                parts[2 * n, H[h]] = part[:, :LANES].astype(BF16)
                parts[2 * n + 1, H[h]] = part[:, LANES:].astype(BF16)

    def own_at(y_new):
        return x_hi * NY + y_new

    def far_at(y_new):
        return (1 - x_hi) * NY + y_new

    def plus(first, second):
        return (first.astype(F32) + second.astype(F32)).astype(BF16)

    def key_far_start(role):
        plus_block, minus_block = ((ym, yp), (yp, ym))[role]
        send(("g_p", role), parts.at[far_at(plus_block), H[1]], gin.at[role, 1], dev_yp)
        send(("g_m", role), parts.at[far_at(minus_block), H[0]], gin.at[role, 0], dev_ym)

    def key_cross(role, h):
        block = far_at((y2, y)[role])
        arrive((("g_m", "g_p")[h], role), gin.at[role, h])
        xout[role, h] = plus(gin[role, h], parts[block, H[h]])
        send(("x", role, h), xout.at[role, h], cin.at[role, h], dev_far)

    def key_own_start():
        send("d1p", parts.at[own_at(yp), H[1]], near.at[0, H[1]], dev_yp)
        send("d1m", parts.at[own_at(ym), H[0]], near.at[1, H[0]], dev_ym)

    def key_two_away(way):
        arrive(("x", 0, way), cin.at[0, way])
        two_out[way] = plus(cin[0, way], parts[own_at(y2), H[way]])
        send(("d2", way), two_out.at[way], merge_in.at[way], ways[way])

    def key_merge(way):
        arrive(("d2", way), merge_in.at[way])
        merge_out[way] = plus(merge_in[way], parts[own_at((yp, ym)[way]), H[way]])
        send(("d1", way), merge_out.at[way], near.at[way, H[way]], ways[way])

    def key_end():
        arrive("d1p", near.at[0, H[1]])
        arrive("d1m", near.at[1, H[0]])
        for h in range(2):
            arrive(("x", 1, h), cin.at[1, h])
        for h in range(2):
            arrive(("d1", h), near.at[h, H[h]])
            total = parts[own_at(y), H[h]].astype(F32) + cin[1, h].astype(F32)
            total = total + (near[0, H[h]].astype(F32) + near[1, H[h]].astype(F32))
            keys_ref[H[h], :] = (total * inv_col[H[h], :]).astype(BF16)

    def weight_grad_side(x_side):
        @pl.loop(0, 2)
        def _(k):
            p = x_side * 2 + k
            rhs = jnp.concatenate([cotg[2 * p], cotg[2 * p + 1]], axis=1)
            cols = pl.ds(pl.multiple_of(p * 2 * LANES, LANES), 2 * LANES)
            for h in range(2):
                rows = slice(h * (feats // 2), (h + 1) * (feats // 2))
                wgrad_ref[rows, cols] = jnp.dot(
                    normed_t[rows, :], rhs, preferred_element_type=F32
                ).astype(BF16)

    def normed_grads(first, last):
        step = 2 * LANES

        steps = tokens_n // step

        @pl.loop(first * steps // 4, last * steps // 4)
        def _(m):
            rows = pl.ds(pl.multiple_of(m * step, step), step)
            lhs = jnp.concatenate([cotg[k, rows, :] for k in range(GROUP)], axis=1)
            d = lax.dot_general(
                lhs, wt[...], (((1,), (1,)), ((), ())), preferred_element_type=F32
            )
            d = d * gain[...]
            dscaled[rows, :] = d
            acc = jnp.zeros((step, LANES), F32)
            for j in range(fblocks):
                cols = slice(j * LANES, (j + 1) * LANES)
                acc = acc + d[:, cols] * tok[rows, cols].astype(F32)
            for k in range(step // LANES):
                projs[t, pl.ds(m * (step // LANES) + k, 1), :] = lane_sum_row(
                    acc[k * LANES : (k + 1) * LANES]
                )

    def proj_send():
        for d in range(1, GROUP):
            send(("proj", d), projs.at[t], projs.at[t], (r, (t + d) % GROUP))

    def proj_end():
        for d in range(1, GROUP):
            arrive(("proj", d), projs.at[(t + GROUP - d) % GROUP])
        total = projs[0]
        for k in range(1, GROUP):
            total = total + projs[k]
        projected = total * inv_row[...] / full_width
        rowproj_ref[...] = projected * math.sqrt(full_width)
        other_row[...] = projected * inv_row[...] * inv_row[...]

    def token_grads():
        @pl.loop(0, blocks)
        def _(b):
            rows = rows_of(b)
            column = inv_col[rows, :]
            other = column_of(other_row[pl.ds(b, 1), :])
            for j in range(fblocks):
                cols = slice(j * LANES, (j + 1) * LANES)
                tgrad_ref[rows, cols] = (
                    column * dscaled[rows, cols] - tok[rows, cols].astype(F32) * other
                ).astype(BF16)

    def quantize(first, last):
        if first == 0:
            local["delta"].wait()
        ones_blocks = block_ones()

        @pl.loop(first * zs // 2, last * zs // 2)
        def _(i):
            shares = (2 * i, 2 * i + 1)
            pieces = [
                delta[:, pl.ds(pl.multiple_of(s * share + k * LANES, LANES), LANES)]
                for s in shares
                for k in range(width)
            ]
            values = jnp.concatenate([v.astype(F32) for v in pieces], axis=0).astype(BF16)
            coded = quantized(values, ones_blocks)
            for n, s in enumerate(shares):
                qsend[s % LOCAL, s // LOCAL] = coded[n * width * frag : (n + 1) * width * frag]

    share_rows = qsend.shape[2]
    cut = share_rows // 32 * 16
    pieces = (slice(0, share_rows - cut), slice(share_rows - cut, share_rows))
    far_first = sorted(range(1, zs), key=lambda d: -min(d, zs - d))

    def delta_start(i):
        p = pieces[i]
        for d in (2, 1, 3):
            to = (e + d) % LOCAL
            send(("r1", i, d), qsend.at[to, :, p], r1.at[e, :, p], of_local(z, to))

    def delta_sum(i):
        p = pieces[i]
        r1[e, :, p, :] = qsend[e, :, p, :]
        for d in range(1, LOCAL):
            arrive(("r1", i, d), r1.at[(e + LOCAL - d) % LOCAL, :, p])

        @pl.loop(0, zs)
        def _(k):
            s1[k, p, :] = (r1[0, k, p, :].astype(F32) + r1[1, k, p, :].astype(F32)) + (
                r1[2, k, p, :].astype(F32) + r1[3, k, p, :].astype(F32)
            )

        r2[z, p, :] = s1[z, p, :]

    def delta_z(i):
        p = pieces[i]
        for d in far_first:
            to = (z + d) % zs
            send(("r2", i, d), s1.at[to, p], r2.at[z, p], of_local(to, e))

    def delta_average(i):
        p = pieces[i]
        for d in range(1, zs):
            arrive(("r2", i, d), r2.at[(z + zs - d) % zs, p])
        total = r2[0, p, :]
        for k in range(1, zs):
            total = total + r2[k, p, :]
        upd[e, z, p, :] = quantized(total / (LOCAL * zs), block_ones()).astype(BF16)
        for d in far_first:
            send(("r3", i, d), upd.at[e, z, p], upd.at[e, z, p], of_local((z + d) % zs, e))

    def update_local(i):
        p = pieces[i]
        for d in range(1, zs):
            arrive(("r3", i, d), upd.at[e, (z + zs - d) % zs, p])
        send(("r4x", i), upd.at[e, :, p], upd.at[e, :, p], of_local(z, e_xlo))
        send(("r4c", i), upd.at[e, :, p], upd.at[e, :, p], of_local(z, e_core))

    def update_core(i):
        p = pieces[i]
        arrive(("r4x", i), upd.at[e_xlo, :, p])
        send(("r4xc", i), upd.at[e_xlo, :, p], upd.at[e_xlo, :, p], of_local(z, e_core))

    def update_end():
        for i, p in enumerate(pieces):
            arrive(("r4c", i), upd.at[e_core, :, p])
            arrive(("r4xc", i), upd.at[e_diag, :, p])

        @pl.loop(0, LOCAL * zs)
        def _(s):
            value = upd[s % LOCAL, s // LOCAL].astype(F32)
            for k in range(width):
                cols = pl.ds(pl.multiple_of(s * share + k * LANES, LANES), LANES)
                update_ref[:, cols] = value[k * frag : (k + 1) * frag, :]

    load()
    greet()
    quantize(0, 4)
    meet()
    delta_start(0)
    cot_start(0)
    cot_start(1)
    delta_start(1)
    sum_squares()
    weight_ready()
    key_parts(1 - x_hi)
    key_far_start(0)
    sum_squares_send()
    cot_onward(0)
    cot_onward(1)
    cot_far_start(0)
    delta_sum(0)
    meet_z()
    delta_z(0)
    key_cross(0, 0)
    key_cross(0, 1)
    key_far_start(1)
    delta_sum(1)
    delta_z(1)
    sum_squares_end()
    normed_rows()
    key_parts(x_hi)
    cot_far_start(1)
    cot_own_end()
    key_two_away(0)
    key_two_away(1)
    delta_average(0)
    key_cross(1, 0)
    cot_far_onward(0)
    key_cross(1, 1)
    cot_far_onward(1)
    delta_average(1)
    key_merge(0)
    key_merge(1)
    key_own_start()
    weight_grad_side(x_hi)
    update_local(0)
    cot_far_end()
    normed_grads(0, 4)
    proj_send()
    update_local(1)
    weight_grad_side(1 - x_hi)
    update_core(0)
    update_core(1)
    key_end()
    proj_end()
    token_grads()
    update_end()

    for copy in pending:
        copy.wait_send()


def finish_kernel(
    keys_ref,
    tgrad_ref,
    rowproj_ref,
    wgrad_ref,
    update_ref,
    params_ref,
    momentum_ref,
    keys_hbm,
    tgrad_hbm,
    rowproj_hbm,
    wgrad_hbm,
    params_hbm,
    momentum_hbm,
    new_params,
    new_momentum,
    sem,
):
    moves = [
        (wgrad_ref, wgrad_hbm),
        (tgrad_ref, tgrad_hbm),
        (keys_ref, keys_hbm),
        (rowproj_ref, rowproj_hbm),
    ]
    copies = [pltpu.make_async_copy(a, b, sem.at[i]) for i, (a, b) in enumerate(moves)]
    for copy in copies:
        copy.start()
    rows, columns = new_params.shape
    parts = 4
    step = columns // parts
    for k in range(parts):
        cols = pl.ds(k * step, step)

        @pl.loop(0, rows // 8)
        def _(b):
            at = (pl.ds(pl.multiple_of(b * 8, 8), 8), cols)
            update = update_ref[at]
            moved = OUTER_MOMENTUM * momentum_ref[at] + update
            new_momentum[at] = moved
            new_params[at] = params_ref[at] - OUTER_RATE * (update + OUTER_MOMENTUM * moved)

        for j, (a, b) in enumerate(((new_params, params_hbm), (new_momentum, momentum_hbm))):
            copy = pltpu.make_async_copy(
                a.at[:, cols], b.at[:, cols], sem.at[len(moves) + 2 * k + j]
            )
            copy.start()
            copies.append(copy)
    for copy in copies:
        copy.wait()


def per_device(tokens, norm_gain, key_weight, key_cotangent, local_delta, outer_params, momentum):
    tok_n, feats = tokens.shape
    heads = key_weight.shape[1]
    full_width = feats * lax.axis_size("tensor")
    workers = lax.axis_size("replica")
    zs = workers // LOCAL
    frag, row_width = outer_params.shape
    share_rows = frag * row_width // workers // LANES
    half = tok_n // 2
    kb = key_cotangent.shape[1]
    hbm = pl.BlockSpec(memory_space=pltpu.HBM)
    vmem = pl.BlockSpec(memory_space=pltpu.VMEM)
    blocks = tok_n // LANES
    operands = (tokens, norm_gain.reshape(1, feats), key_weight, key_cotangent, local_delta[0])
    keys, tgrad, rowproj, wgrad, update = pl.pallas_call(
        functools.partial(kernel, full_width),
        out_shape=(
            jax.ShapeDtypeStruct((tok_n, kb), BF16),
            jax.ShapeDtypeStruct((tok_n, feats), BF16),
            jax.ShapeDtypeStruct((blocks, LANES), F32),
            jax.ShapeDtypeStruct((feats, heads), BF16),
            jax.ShapeDtypeStruct((frag, row_width), F32),
        ),
        in_specs=[hbm] * 5,
        out_specs=(vmem,) * 5,
        scratch_shapes=[
            pltpu.VMEM((tok_n, feats), BF16),
            pltpu.VMEM((1, feats), F32),
            pltpu.VMEM(local_delta.shape[1:], BF16),
            pltpu.VMEM((feats, heads), BF16),
            pltpu.VMEM((tok_n, feats), BF16),
            pltpu.VMEM((feats, tok_n), BF16),
            pltpu.VMEM((GROUP, tok_n, kb), BF16),
            pltpu.VMEM((GROUP, tok_n, kb), BF16),
            pltpu.VMEM((tok_n, feats), F32),
            pltpu.VMEM((tok_n, LANES), F32),
            pltpu.VMEM((blocks, LANES), F32),
            pltpu.VMEM((blocks, LANES), F32),
            pltpu.VMEM((GROUP, blocks, LANES), F32),
            pltpu.VMEM((GROUP, blocks, LANES), F32),
            pltpu.VMEM((2, 2, half, kb), BF16),
            pltpu.VMEM((2, 2, half, kb), BF16),
            pltpu.VMEM((2, 2, half, kb), BF16),
            pltpu.VMEM((2, half, kb), BF16),
            pltpu.VMEM((2, half, kb), BF16),
            pltpu.VMEM((2, half, kb), BF16),
            pltpu.VMEM((2, tok_n, kb), BF16),
            pltpu.VMEM((LOCAL, zs, share_rows, LANES), BF16),
            pltpu.VMEM((LOCAL, zs, share_rows, LANES), BF16),
            pltpu.VMEM((zs, share_rows, LANES), F32),
            pltpu.VMEM((zs, share_rows, LANES), F32),
            pltpu.VMEM((LOCAL, zs, share_rows, LANES), BF16),
            pltpu.SemaphoreType.REGULAR((2,)),
            pltpu.SemaphoreType.DMA((N_REMOTE,)),
            pltpu.SemaphoreType.DMA((N_REMOTE,)),
            pltpu.SemaphoreType.DMA((N_LOCAL,)),
        ],
        compiler_params=pltpu.CompilerParams(
            collective_id=0, has_side_effects=True, vmem_limit_bytes=44 * 1024 * 1024
        ),
        cost_estimate=pl.CostEstimate(
            flops=6 * tok_n * feats * heads, bytes_accessed=16 * 1024 * 1024, transcendentals=0
        ),
    )(*(pltpu.with_memory_space_constraint(a, pltpu.HBM) for a in operands))
    keys, tgrad, rowproj, wgrad, new_params, new_momentum = pl.pallas_call(
        finish_kernel,
        out_shape=(
            jax.ShapeDtypeStruct((tok_n, kb), BF16),
            jax.ShapeDtypeStruct((tok_n, feats), BF16),
            jax.ShapeDtypeStruct((blocks, LANES), F32),
            jax.ShapeDtypeStruct((feats, heads), BF16),
            jax.ShapeDtypeStruct((frag, row_width), F32),
            jax.ShapeDtypeStruct((frag, row_width), F32),
        ),
        in_specs=[vmem] * 7,
        out_specs=(hbm,) * 6,
        scratch_shapes=[
            pltpu.VMEM((frag, row_width), F32),
            pltpu.VMEM((frag, row_width), F32),
            pltpu.SemaphoreType.DMA((12,)),
        ],
        compiler_params=pltpu.CompilerParams(vmem_limit_bytes=16 * 1024 * 1024),
        cost_estimate=pl.CostEstimate(
            flops=8 * frag * row_width, bytes_accessed=8 * 1024 * 1024, transcendentals=0
        ),
    )(keys, tgrad, rowproj, wgrad, update, outer_params, momentum)
    return (keys, tgrad, rowproj.reshape(tok_n), wgrad[None], new_params, new_momentum)


def solution(mesh):
    placed = (
        P("replica", "tensor"),
        P("tensor"),
        P("tensor", None),
        P("replica", "tensor"),
        P("replica", "tensor", None),
        P("tensor", None),
        P("tensor", None),
    )
    return jax.shard_map(
        per_device,
        mesh=mesh,
        in_specs=placed,
        out_specs=(
            P("replica", "tensor"),
            P("replica", "tensor"),
            P("replica"),
            P("replica", "tensor", None),
            P("tensor", None),
            P("tensor", None),
        ),
        check_vma=False,
    )
```

```python
import functools
import math

import jax
import jax.numpy as jnp
from jax import lax
from jax.experimental import pallas as pl
from jax.experimental.pallas import tpu as pltpu
from jax.sharding import PartitionSpec as P

SCALE_LOWEST = -7
SCALE_HIGHEST = 1
OUTER_RATE = 0.7
OUTER_MOMENTUM = 0.9
EPSILON = 1e-05
GRID_EDGES = (
    (0.25, 0.5, False),
    (0.75, 0.5, True),
    (1.25, 0.5, False),
    (1.75, 0.5, True),
    (2.5, 1.0, False),
    (3.5, 1.0, True),
    (5.0, 2.0, False),
)
MESH = pl.DeviceIdType.MESH
LANES = 128
NY = 4
GROUP = 8
LOCAL = 4
N_REMOTE = 112
N_LOCAL = 16
F32 = jnp.float32
BF16 = jnp.bfloat16


def quantized(values, ones_blocks):
    kind = values.dtype
    magnitude = jnp.abs(values)

    def const(value):
        return jnp.full(values.shape, value, kind)

    weight = const(1.0)
    for exponent in range(SCALE_LOWEST, SCALE_HIGHEST):
        weight = jnp.where(
            magnitude > const(6.0 * 2.0**exponent),
            const(64.0 ** (exponent - SCALE_LOWEST + 1)),
            weight,
        )
    total = jnp.dot(weight.astype(BF16), ones_blocks, preferred_element_type=F32).astype(kind)
    scale = const(2.0**SCALE_LOWEST)
    back = const(2.0**-SCALE_LOWEST)
    for exponent in range(SCALE_LOWEST, SCALE_HIGHEST):
        above = total >= const(64.0 ** (exponent - SCALE_LOWEST + 1))
        scale = jnp.where(above, const(2.0 ** (exponent + 1)), scale)
        back = jnp.where(above, const(2.0 ** -(exponent + 1)), back)
    ratio = magnitude * back
    level = const(0.0)
    reached = 0.0
    for edge, step, upward in GRID_EDGES:
        reached += step
        passed = ratio >= const(edge) if upward else ratio > const(edge)
        level = jnp.where(passed, const(reached), level)
    level = level * scale
    return jnp.where(values < const(0.0), -level, level)


def weight_grad_pair(pair, cotg, normed_t, out):
    rhs = jnp.concatenate([cotg[2 * pair], cotg[2 * pair + 1]], axis=1)
    cols = pl.ds(pl.multiple_of(pair * 2 * LANES, LANES), 2 * LANES)
    feats = normed_t.shape[0]
    for h in range(2):
        rows = slice(h * (feats // 2), (h + 1) * (feats // 2))
        out[rows, cols] = jnp.dot(
            normed_t[rows, :], rhs, preferred_element_type=F32
        ).astype(BF16)


def block_ones():
    row = lax.broadcasted_iota(jnp.int32, (LANES, LANES), 0) // 32
    column = lax.broadcasted_iota(jnp.int32, (LANES, LANES), 1) // 32
    return jnp.where(row == column, 1.0, 0.0).astype(BF16)


def kernel(
    full_width,
    tok_hbm,
    gain_hbm,
    weight_hbm,
    cot_hbm,
    delta_hbm,
    keys_ref,
    tgrad_ref,
    rowproj_ref,
    wgrad_ref,
    upd,
    cotg,
    normed_t,
    tok,
    gain,
    delta,
    wt,
    scaled,
    parts,
    dpart,
    inv_col,
    inv_row,
    other_row,
    sums,
    projs,
    half_proj,
    gin,
    xout,
    cin,
    two_out,
    merge_in,
    merge_out,
    near,
    qsend,
    r1,
    s1,
    r2,
    ready,
    ssem,
    rsem,
    lsem,
):
    r = lax.axis_index("replica")
    t = lax.axis_index("tensor")
    zs = lax.axis_size("replica") // LOCAL
    core = r % 2
    x_lo = (r // 2) % 2
    z = r // LOCAL
    x_hi = t // NY
    y = t % NY
    tokens_n, feats = tok.shape
    half = tokens_n // 2
    H = (pl.ds(0, half), pl.ds(half, half))
    yp, ym, y2 = (y + 1) % NY, (y + 3) % NY, (y + 2) % NY
    e = core * 2 + x_lo
    e_xlo = core * 2 + (1 - x_lo)
    e_core = (1 - core) * 2 + x_lo
    e_diag = (1 - core) * 2 + (1 - x_lo)

    def of_local(z_new, e_new):
        return ((z_new * 2 + e_new % 2) * 2 + e_new // 2, t)

    dev_yp = (r, x_hi * NY + yp)
    dev_ym = (r, x_hi * NY + ym)
    ways = (dev_yp, dev_ym)
    t_far = (1 - x_hi) * NY + y
    dev_far = (r, t_far)

    names = {}
    pending = []

    def index_of(name):
        return names.setdefault(name, len(names))

    def send(name, src, dst, device):
        i = index_of(name)
        copy = pltpu.make_async_remote_copy(
            src_ref=src,
            dst_ref=dst,
            send_sem=ssem.at[i],
            recv_sem=rsem.at[i],
            device_id=device,
            device_id_type=MESH,
        )
        copy.start()
        pending.append(copy)

    def arrive(name, landing):
        i = index_of(name)
        pltpu.make_async_remote_copy(
            src_ref=landing,
            dst_ref=landing,
            send_sem=ssem.at[i],
            recv_sem=rsem.at[i],
            device_id=dev_yp,
            device_id_type=MESH,
        ).wait_recv()

    local = {}

    def fetch(name, src, dst):
        i = len(local)
        copy = pltpu.make_async_copy(src, dst, lsem.at[i])
        copy.start()
        local[name] = copy

    blocks = tokens_n // LANES
    fblocks = feats // LANES
    share = delta.shape[1] // (LOCAL * zs)
    frag = delta.shape[0]
    width = share // LANES
    t_ym, t_yp, t_y2 = x_hi * NY + ym, x_hi * NY + yp, x_hi * NY + y2
    f_ym, f_yp, f_y2 = ((1 - x_hi) * NY + k for k in (ym, yp, y2))

    def rows_of(b):
        return pl.ds(pl.multiple_of(b * LANES, LANES), LANES)

    def lane_sum_row(acc):
        return jnp.sum(acc.T, axis=0, keepdims=True)

    def column_of(row):
        return jnp.broadcast_to(row, (LANES, LANES)).T

    def load():
        fetch("delta", delta_hbm, delta)
        fetch("gain", gain_hbm, gain)
        for h in range(2):
            fetch(("tok", h), tok_hbm.at[H[h]], tok.at[H[h]])
        fetch("weight", weight_hbm, wt)
        fetch("cot", cot_hbm, cotg.at[t])

    far_first = sorted(range(1, zs), key=lambda d: -min(d, zs - d))

    def tell(device):
        pl.semaphore_signal(
            pltpu.get_barrier_semaphore(), inc=1, device_id=device, device_id_type=MESH
        )

    def greet():
        for d in range(1, GROUP):
            tell((r - core, (t + d) % GROUP))
        tell(of_local(z, 1 - x_lo))

        @pl.when(core == 1)
        def _():
            tell(of_local(z, x_lo))

    def greet_z():
        for d in far_first:
            tell(of_local((z + d) % zs, 2))
            tell(of_local((z + d) % zs, 3))

    def collect(collector, count, ready_sem):
        @pl.when(core == collector)
        def _():
            pl.semaphore_wait(pltpu.get_barrier_semaphore(), count)
            pl.semaphore_signal(
                ready_sem, inc=1, device_id=of_local(z, e_core), device_id_type=MESH
            )

        @pl.when(core != collector)
        def _():
            pl.semaphore_wait(ready_sem, 1)

    def meet():
        collect(0, 2 * GROUP + 1, ready.at[0])

    def meet_z():
        collect(1, LOCAL * (zs - 1), ready.at[1])

    def cot_start(i):
        h, k = H[i], H[1 - i]
        send(("own_p", i), cot_hbm.at[h], cotg.at[t, h], dev_yp)
        send(("own_m", 1 - i), cot_hbm.at[k], cotg.at[t, k], dev_ym)
        send(("c", i), cot_hbm.at[h], cotg.at[t, h], dev_far)

    def cot_onward(way):
        block = (t_ym, t_yp)[way]
        arrive((("own_p", "own_m")[way], way), cotg.at[block, H[way]])
        send(("own_on", way), cotg.at[block, H[way]], cotg.at[block, H[way]], ways[way])

    def cot_far_start(h):
        arrive(("c", h), cotg.at[t_far, H[h]])
        send(("far_p", h), cotg.at[t_far, H[h]], cotg.at[t_far, H[h]], dev_yp)
        send(("far_m", h), cotg.at[t_far, H[h]], cotg.at[t_far, H[h]], dev_ym)

    def cot_far_onward(way):
        block = (f_ym, f_yp)[way]
        arrive((("far_p", "far_m")[way], way), cotg.at[block, H[way]])
        send(("far_on", way), cotg.at[block, H[way]], cotg.at[block, H[way]], ways[way])

    def cot_own_end():
        local["cot"].wait()
        arrive(("own_p", 1), cotg.at[t_ym, H[1]])
        arrive(("own_m", 0), cotg.at[t_yp, H[0]])
        arrive(("own_on", 0), cotg.at[t_y2, H[0]])
        arrive(("own_on", 1), cotg.at[t_y2, H[1]])

    def cot_far_end():
        arrive(("far_m", 0), cotg.at[f_yp, H[0]])
        arrive(("far_p", 1), cotg.at[f_ym, H[1]])
        arrive(("far_on", 0), cotg.at[f_y2, H[0]])
        arrive(("far_on", 1), cotg.at[f_y2, H[1]])

    def sum_squares():
        def one(b):
            rows = rows_of(b)
            acc = jnp.zeros((LANES, LANES), F32)
            for j in range(fblocks):
                cols = slice(j * LANES, (j + 1) * LANES)
                v = tok[rows, cols].astype(F32)
                acc = acc + v * v
                scaled[rows, cols] = (v * gain[:, cols]).astype(BF16)
            sums[t, pl.ds(b, 1), :] = lane_sum_row(acc)

        local["gain"].wait()
        for h in range(2):
            local[("tok", h)].wait()
            pl.loop(h * blocks // 2, (h + 1) * blocks // 2)(one)

    def sum_squares_send():
        for d in range(1, GROUP):
            send(("sum", d), sums.at[t], sums.at[t], (r, (t + d) % GROUP))

    def sum_squares_end():
        for d in range(1, GROUP):
            arrive(("sum", d), sums.at[(t + GROUP - d) % GROUP])
        total = sums[0]
        for k in range(1, GROUP):
            total = total + sums[k]
        inv_row[...] = lax.rsqrt(total / full_width + EPSILON)

    def normed_rows(first, last):
        @pl.loop(first * blocks // 2, last * blocks // 2)
        def _(b):
            rows = rows_of(b)
            column = column_of(inv_row[pl.ds(b, 1), :])
            inv_col[rows, :] = column
            for j in range(fblocks):
                cols = slice(j * LANES, (j + 1) * LANES)
                value = (tok[rows, cols].astype(F32) * column * gain[:, cols]).astype(BF16)
                normed_t[cols, rows] = value.T

    def weight_ready():
        local["weight"].wait()

    def key_parts(x_side):
        @pl.loop(0, 2)
        def _(k):
            n = x_side * 2 + k
            cols = pl.ds(pl.multiple_of(n * 2 * LANES, LANES), 2 * LANES)
            for h in range(2):
                part = jnp.dot(scaled[H[h], :], wt[:, cols], preferred_element_type=F32)
                parts[2 * n, H[h]] = part[:, :LANES].astype(BF16)
                parts[2 * n + 1, H[h]] = part[:, LANES:].astype(BF16)

    def own_at(y_new):
        return x_hi * NY + y_new

    def far_at(y_new):
        return (1 - x_hi) * NY + y_new

    def plus(first, second):
        return (first.astype(F32) + second.astype(F32)).astype(BF16)

    def key_far_start(role):
        plus_block, minus_block = ((ym, yp), (yp, ym))[role]
        send(("g_p", role), parts.at[far_at(plus_block), H[1]], gin.at[role, 1], dev_yp)
        send(("g_m", role), parts.at[far_at(minus_block), H[0]], gin.at[role, 0], dev_ym)

    def key_cross(role, h):
        block = far_at((y2, y)[role])
        arrive((("g_m", "g_p")[h], role), gin.at[role, h])
        xout[role, h] = plus(gin[role, h], parts[block, H[h]])
        send(("x", role, h), xout.at[role, h], cin.at[role, h], dev_far)

    def key_own_start():
        send("d1p", parts.at[own_at(yp), H[1]], near.at[0, H[1]], dev_yp)
        send("d1m", parts.at[own_at(ym), H[0]], near.at[1, H[0]], dev_ym)

    def key_two_away(way):
        arrive(("x", 0, way), cin.at[0, way])
        two_out[way] = plus(cin[0, way], parts[own_at(y2), H[way]])
        send(("d2", way), two_out.at[way], merge_in.at[way], ways[way])

    def key_merge(way):
        arrive(("d2", way), merge_in.at[way])
        merge_out[way] = plus(merge_in[way], parts[own_at((yp, ym)[way]), H[way]])
        send(("d1", way), merge_out.at[way], near.at[way, H[way]], ways[way])

    def key_end():
        arrive("d1p", near.at[0, H[1]])
        arrive("d1m", near.at[1, H[0]])
        for h in range(2):
            arrive(("x", 1, h), cin.at[1, h])
        for h in range(2):
            arrive(("d1", h), near.at[h, H[h]])
            total = parts[own_at(y), H[h]].astype(F32) + cin[1, h].astype(F32)
            total = total + (near[0, H[h]].astype(F32) + near[1, H[h]].astype(F32))
            keys_ref[H[h], :] = (total * inv_col[H[h], :]).astype(BF16)

    def weight_grad(first, last):
        @pl.loop(first, last)
        def _(k):
            weight_grad_pair(x_hi * 2 + k, cotg, normed_t, wgrad_ref)

    def project(x_side):
        @pl.loop(0, blocks)
        def _(b):
            rows = rows_of(b)
            acc = jnp.zeros((LANES, LANES), F32)
            for k in range(NY):
                block = x_side * NY + k
                acc = acc + cotg[block, rows, :].astype(F32) * parts[block, rows, :].astype(F32)
            half_proj[x_side, pl.ds(b, 1), :] = lane_sum_row(acc)

    step = 2 * LANES
    steps = tokens_n // step

    def cot_times_weight(x_side, rows):
        lhs = jnp.concatenate([cotg[x_side * NY + k, rows, :] for k in range(NY)], axis=1)
        cols = pl.ds(pl.multiple_of(x_side * NY * LANES, LANES), NY * LANES)
        return lax.dot_general(
            lhs, wt[:, cols], (((1,), (1,)), ((), ())), preferred_element_type=F32
        )

    def normed_grads_own(first, last):
        @pl.loop(first * steps // 4, last * steps // 4)
        def _(m):
            rows = pl.ds(pl.multiple_of(m * step, step), step)
            dpart[rows, :] = cot_times_weight(x_hi, rows)

    def proj_send():
        projs[t] = half_proj[0] + half_proj[1]
        for d in range(1, GROUP):
            send(("proj", d), projs.at[t], projs.at[t], (r, (t + d) % GROUP))

    def proj_end():
        for d in range(1, GROUP):
            arrive(("proj", d), projs.at[(t + GROUP - d) % GROUP])
        total = projs[0]
        for k in range(1, GROUP):
            total = total + projs[k]
        projected = total * inv_row[...] / full_width
        rowproj_ref[...] = projected * math.sqrt(full_width)
        other_row[...] = projected * inv_row[...] * inv_row[...]

    def token_grads(first, last):
        @pl.loop(first * steps // 4, last * steps // 4)
        def _(m):
            rows = pl.ds(pl.multiple_of(m * step, step), step)
            d = dpart[rows, :] + cot_times_weight(1 - x_hi, rows)
            column = inv_col[rows, :]
            other = jnp.concatenate(
                [column_of(other_row[pl.ds(2 * m + k, 1), :]) for k in range(2)], axis=0
            )
            for j in range(fblocks):
                cols = slice(j * LANES, (j + 1) * LANES)
                tgrad_ref[rows, cols] = (
                    column * (d[:, cols] * gain[:, cols]) - tok[rows, cols].astype(F32) * other
                ).astype(BF16)

    def quantize(first, last):
        if first == 0:
            local["delta"].wait()
        ones_blocks = block_ones()

        @pl.loop(first * zs // 2, last * zs // 2)
        def _(i):
            shares = (2 * i, 2 * i + 1)
            pieces = [
                delta[:, pl.ds(pl.multiple_of(s * share + k * LANES, LANES), LANES)]
                for s in shares
                for k in range(width)
            ]
            values = jnp.concatenate([v.astype(F32) for v in pieces], axis=0).astype(BF16)
            coded = quantized(values, ones_blocks)
            for n, s in enumerate(shares):
                qsend[s % LOCAL, s // LOCAL] = coded[n * width * frag : (n + 1) * width * frag]

    share_rows = qsend.shape[2]
    cut = share_rows // 32 * 16
    pieces = (slice(0, share_rows - cut), slice(share_rows - cut, share_rows))

    def delta_start(i):
        p = pieces[i]
        for d in (2, 1, 3):
            to = (e + d) % LOCAL
            send(("r1", i, d), qsend.at[to, :, p], r1.at[e, :, p], of_local(z, to))

    def delta_sum(i):
        p = pieces[i]
        r1[e, :, p, :] = qsend[e, :, p, :]
        for d in range(1, LOCAL):
            arrive(("r1", i, d), r1.at[(e + LOCAL - d) % LOCAL, :, p])

        @pl.loop(0, zs)
        def _(k):
            s1[k, p, :] = (r1[0, k, p, :].astype(F32) + r1[1, k, p, :].astype(F32)) + (
                r1[2, k, p, :].astype(F32) + r1[3, k, p, :].astype(F32)
            )

        r2[z, p, :] = s1[z, p, :]

    def delta_z(i):
        p = pieces[i]
        for d in far_first:
            to = (z + d) % zs
            send(("r2", i, d), s1.at[to, p], r2.at[z, p], of_local(to, e))

    def delta_average(i):
        p = pieces[i]
        for d in range(1, zs):
            arrive(("r2", i, d), r2.at[(z + zs - d) % zs, p])
        total = r2[0, p, :]
        for k in range(1, zs):
            total = total + r2[k, p, :]
        upd[e, z, p, :] = quantized(total / (LOCAL * zs), block_ones()).astype(BF16)
        mine = upd.at[e, z, p]
        for d in (*far_first, 0):
            send(("r3x", i, d), mine, mine, of_local((z + d) % zs, e_xlo))
        for d in far_first:
            send(("r3", i, d), mine, mine, of_local((z + d) % zs, e))

    def update_core(i):
        p = pieces[i]
        for d in range(zs):
            arrive(("r3x", i, d), upd.at[e_xlo, (z + zs - d) % zs, p])
        for d in range(1, zs):
            arrive(("r3", i, d), upd.at[e, (z + zs - d) % zs, p])
        both = upd.at[pl.ds(core * 2, 2), :, p]
        send(("r4", i), both, both, of_local(z, e_core))

    def update_end():
        for i, p in enumerate(pieces):
            arrive(("r4", i), upd.at[pl.ds((1 - core) * 2, 2), :, p])

    greet()
    load()
    meet()
    cot_start(0)
    greet_z()
    cot_start(1)
    quantize(0, 4)
    delta_start(0)
    delta_start(1)
    sum_squares()
    weight_ready()
    key_parts(1 - x_hi)
    key_far_start(0)
    sum_squares_send()
    cot_onward(0)
    cot_onward(1)
    cot_far_start(0)
    key_parts(x_hi)
    delta_sum(0)
    meet_z()
    delta_z(0)
    key_cross(0, 0)
    key_cross(0, 1)
    cot_far_start(1)
    key_far_start(1)
    delta_sum(1)
    delta_z(1)
    sum_squares_end()
    normed_rows(0, 2)
    key_two_away(0)
    key_two_away(1)
    cot_own_end()
    project(x_hi)
    cot_far_onward(0)
    cot_far_onward(1)
    delta_average(0)
    key_own_start()
    key_cross(1, 0)
    key_cross(1, 1)
    delta_average(1)
    key_merge(0)
    key_merge(1)
    weight_grad(0, 1)
    cot_far_end()
    project(1 - x_hi)
    proj_send()
    weight_grad(1, 2)
    normed_grads_own(0, 4)
    proj_end()
    update_core(0)
    token_grads(0, 2)
    update_core(1)
    token_grads(2, 4)
    key_end()
    update_end()

    for copy in pending:
        copy.wait_send()


def finish_kernel(
    keys_ref,
    tgrad_ref,
    rowproj_ref,
    wgrad_ref,
    upd_ref,
    cotg_ref,
    normed_t_ref,
    params_ref,
    momentum_ref,
    keys_hbm,
    tgrad_hbm,
    rowproj_hbm,
    wgrad_hbm,
    params_hbm,
    momentum_hbm,
    wgrad_far,
    new_params,
    new_momentum,
    sem,
):
    x_hi = lax.axis_index("tensor") // NY
    heads = wgrad_ref.shape[1]
    own = pl.ds(pl.multiple_of(x_hi * (heads // 2), LANES), heads // 2)
    copies = []

    def write(src, dst):
        copy = pltpu.make_async_copy(src, dst, sem.at[len(copies)])
        copy.start()
        copies.append(copy)

    write(tgrad_ref, tgrad_hbm)
    write(wgrad_ref.at[:, own], wgrad_hbm.at[:, own])
    write(keys_ref, keys_hbm)
    write(rowproj_ref, rowproj_hbm)

    rows, columns = new_params.shape
    zs = upd_ref.shape[1]
    share = columns // (LOCAL * zs)
    groups = 4 if zs % 4 == 0 else 1
    for g in range(groups):

        @pl.loop(g * LOCAL * zs // groups, (g + 1) * LOCAL * zs // groups)
        def _(s):
            update = upd_ref[s % LOCAL, s // LOCAL].astype(F32)
            for k in range(share // LANES):
                cols = pl.ds(pl.multiple_of(s * share + k * LANES, LANES), LANES)
                piece = update[k * rows : (k + 1) * rows, :]
                moved = OUTER_MOMENTUM * momentum_ref[:, cols] + piece
                new_momentum[:, cols] = moved
                new_params[:, cols] = params_ref[:, cols] - OUTER_RATE * (
                    piece + OUTER_MOMENTUM * moved
                )

        cols = pl.ds(g * (columns // groups), columns // groups)
        write(new_params.at[:, cols], params_hbm.at[:, cols])
        write(new_momentum.at[:, cols], momentum_hbm.at[:, cols])

    for k in range(2):
        pair = (1 - x_hi) * 2 + k
        weight_grad_pair(pair, cotg_ref, normed_t_ref, wgrad_far)
        cols = pl.ds(pl.multiple_of(pair * 2 * LANES, LANES), 2 * LANES)
        write(wgrad_far.at[:, cols], wgrad_hbm.at[:, cols])
    for copy in copies:
        copy.wait()


def per_device(tokens, norm_gain, key_weight, key_cotangent, local_delta, outer_params, momentum):
    tok_n, feats = tokens.shape
    heads = key_weight.shape[1]
    full_width = feats * lax.axis_size("tensor")
    workers = lax.axis_size("replica")
    zs = workers // LOCAL
    frag, row_width = outer_params.shape
    share_rows = frag * row_width // workers // LANES
    half = tok_n // 2
    kb = key_cotangent.shape[1]
    hbm = pl.BlockSpec(memory_space=pltpu.HBM)
    vmem = pl.BlockSpec(memory_space=pltpu.VMEM)
    blocks = tok_n // LANES
    operands = (tokens, norm_gain.reshape(1, feats), key_weight, key_cotangent, local_delta[0])
    results = pl.pallas_call(
        functools.partial(kernel, full_width),
        out_shape=(
            jax.ShapeDtypeStruct((tok_n, kb), BF16),
            jax.ShapeDtypeStruct((tok_n, feats), BF16),
            jax.ShapeDtypeStruct((blocks, LANES), F32),
            jax.ShapeDtypeStruct((feats, heads), BF16),
            jax.ShapeDtypeStruct((LOCAL, zs, share_rows, LANES), BF16),
            jax.ShapeDtypeStruct((GROUP, tok_n, kb), BF16),
            jax.ShapeDtypeStruct((feats, tok_n), BF16),
        ),
        in_specs=[hbm] * 5,
        out_specs=(vmem,) * 7,
        scratch_shapes=[
            pltpu.VMEM((tok_n, feats), BF16),
            pltpu.VMEM((1, feats), F32),
            pltpu.VMEM(local_delta.shape[1:], BF16),
            pltpu.VMEM((feats, heads), BF16),
            pltpu.VMEM((tok_n, feats), BF16),
            pltpu.VMEM((GROUP, tok_n, kb), BF16),
            pltpu.VMEM((tok_n, feats), F32),
            pltpu.VMEM((tok_n, LANES), F32),
            pltpu.VMEM((blocks, LANES), F32),
            pltpu.VMEM((blocks, LANES), F32),
            pltpu.VMEM((GROUP, blocks, LANES), F32),
            pltpu.VMEM((GROUP, blocks, LANES), F32),
            pltpu.VMEM((2, blocks, LANES), F32),
            pltpu.VMEM((2, 2, half, kb), BF16),
            pltpu.VMEM((2, 2, half, kb), BF16),
            pltpu.VMEM((2, 2, half, kb), BF16),
            pltpu.VMEM((2, half, kb), BF16),
            pltpu.VMEM((2, half, kb), BF16),
            pltpu.VMEM((2, half, kb), BF16),
            pltpu.VMEM((2, tok_n, kb), BF16),
            pltpu.VMEM((LOCAL, zs, share_rows, LANES), BF16),
            pltpu.VMEM((LOCAL, zs, share_rows, LANES), BF16),
            pltpu.VMEM((zs, share_rows, LANES), F32),
            pltpu.VMEM((zs, share_rows, LANES), F32),
            pltpu.SemaphoreType.REGULAR((2,)),
            pltpu.SemaphoreType.DMA((N_REMOTE,)),
            pltpu.SemaphoreType.DMA((N_REMOTE,)),
            pltpu.SemaphoreType.DMA((N_LOCAL,)),
        ],
        compiler_params=pltpu.CompilerParams(
            collective_id=0, has_side_effects=True, vmem_limit_bytes=36 * 1024 * 1024
        ),
        cost_estimate=pl.CostEstimate(
            flops=6 * tok_n * feats * heads, bytes_accessed=16 * 1024 * 1024, transcendentals=0
        ),
    )(*(pltpu.with_memory_space_constraint(a, pltpu.HBM) for a in operands))
    keys, tgrad, rowproj, wgrad, new_params, new_momentum = pl.pallas_call(
        finish_kernel,
        out_shape=(
            jax.ShapeDtypeStruct((tok_n, kb), BF16),
            jax.ShapeDtypeStruct((tok_n, feats), BF16),
            jax.ShapeDtypeStruct((blocks, LANES), F32),
            jax.ShapeDtypeStruct((feats, heads), BF16),
            jax.ShapeDtypeStruct((frag, row_width), F32),
            jax.ShapeDtypeStruct((frag, row_width), F32),
        ),
        in_specs=[vmem] * 9,
        out_specs=(hbm,) * 6,
        scratch_shapes=[
            pltpu.VMEM((feats, heads), BF16),
            pltpu.VMEM((frag, row_width), F32),
            pltpu.VMEM((frag, row_width), F32),
            pltpu.SemaphoreType.DMA((16,)),
        ],
        compiler_params=pltpu.CompilerParams(vmem_limit_bytes=16 * 1024 * 1024),
        cost_estimate=pl.CostEstimate(
            flops=8 * frag * row_width, bytes_accessed=8 * 1024 * 1024, transcendentals=0
        ),
    )(*results, outer_params, momentum)
    return (keys, tgrad, rowproj.reshape(tok_n), wgrad[None], new_params, new_momentum)


def solution(mesh):
    placed = (
        P("replica", "tensor"),
        P("tensor"),
        P("tensor", None),
        P("replica", "tensor"),
        P("replica", "tensor", None),
        P("tensor", None),
        P("tensor", None),
    )
    return jax.shard_map(
        per_device,
        mesh=mesh,
        in_specs=placed,
        out_specs=(
            P("replica", "tensor"),
            P("replica", "tensor"),
            P("replica"),
            P("replica", "tensor", None),
            P("tensor", None),
            P("tensor", None),
        ),
        check_vma=False,
    )
```

```python
import functools
import math

import jax
import jax.numpy as jnp
from jax import lax
from jax.experimental import pallas as pl
from jax.experimental.pallas import tpu as pltpu
from jax.sharding import PartitionSpec as P

SCALE_LOWEST = -7
SCALE_HIGHEST = 1
OUTER_RATE = 0.7
OUTER_MOMENTUM = 0.9
EPSILON = 1e-05
GRID_EDGES = (
    (0.25, 0.5, False),
    (0.75, 0.5, True),
    (1.25, 0.5, False),
    (1.75, 0.5, True),
    (2.5, 1.0, False),
    (3.5, 1.0, True),
    (5.0, 2.0, False),
)
MESH = pl.DeviceIdType.MESH
LANES = 128
NY = 4
GROUP = 8
LOCAL = 4
N_REMOTE = 112
N_LOCAL = 16
F32 = jnp.float32
BF16 = jnp.bfloat16


def quantized(values, ones_blocks):
    kind = values.dtype
    magnitude = jnp.abs(values)

    def const(value):
        return jnp.full(values.shape, value, kind)

    weight = const(1.0)
    for exponent in range(SCALE_LOWEST, SCALE_HIGHEST):
        weight = jnp.where(
            magnitude > const(6.0 * 2.0**exponent),
            const(64.0 ** (exponent - SCALE_LOWEST + 1)),
            weight,
        )
    total = jnp.dot(weight.astype(BF16), ones_blocks, preferred_element_type=F32).astype(kind)
    scale = const(2.0**SCALE_LOWEST)
    back = const(2.0**-SCALE_LOWEST)
    for exponent in range(SCALE_LOWEST, SCALE_HIGHEST):
        above = total >= const(64.0 ** (exponent - SCALE_LOWEST + 1))
        scale = jnp.where(above, const(2.0 ** (exponent + 1)), scale)
        back = jnp.where(above, const(2.0 ** -(exponent + 1)), back)
    ratio = magnitude * back
    level = const(0.0)
    reached = 0.0
    for edge, step, upward in GRID_EDGES:
        reached += step
        passed = ratio >= const(edge) if upward else ratio > const(edge)
        level = jnp.where(passed, const(reached), level)
    level = level * scale
    return jnp.where(values < const(0.0), -level, level)


def weight_grad_pair(pair, cotg, normed_t, out):
    rhs = jnp.concatenate([cotg[2 * pair], cotg[2 * pair + 1]], axis=1)
    cols = pl.ds(pl.multiple_of(pair * 2 * LANES, LANES), 2 * LANES)
    feats = normed_t.shape[0]
    for h in range(2):
        rows = slice(h * (feats // 2), (h + 1) * (feats // 2))
        out[rows, cols] = jnp.dot(
            normed_t[rows, :], rhs, preferred_element_type=F32
        ).astype(BF16)


def block_ones():
    row = lax.broadcasted_iota(jnp.int32, (LANES, LANES), 0) // 32
    column = lax.broadcasted_iota(jnp.int32, (LANES, LANES), 1) // 32
    return jnp.where(row == column, 1.0, 0.0).astype(BF16)


def kernel(
    full_width,
    tok_hbm,
    gain_hbm,
    weight_hbm,
    cot_hbm,
    delta_hbm,
    keys_ref,
    tgrad_ref,
    rowproj_ref,
    wgrad_ref,
    upd,
    cotg,
    normed_t,
    tok,
    gain,
    delta,
    wt,
    scaled,
    parts,
    dpart,
    inv_col,
    inv_row,
    other_row,
    sums,
    projs,
    half_proj,
    gin,
    xout,
    cin,
    two_out,
    merge_in,
    merge_out,
    near,
    qsend,
    r1,
    s1,
    r2,
    ready,
    ssem,
    rsem,
    lsem,
):
    r = lax.axis_index("replica")
    t = lax.axis_index("tensor")
    zs = lax.axis_size("replica") // LOCAL
    core = r % 2
    x_lo = (r // 2) % 2
    z = r // LOCAL
    x_hi = t // NY
    y = t % NY
    tokens_n, feats = tok.shape
    half = tokens_n // 2
    H = (pl.ds(0, half), pl.ds(half, half))
    yp, ym, y2 = (y + 1) % NY, (y + 3) % NY, (y + 2) % NY
    e = core * 2 + x_lo
    e_xlo = core * 2 + (1 - x_lo)
    e_core = (1 - core) * 2 + x_lo
    e_diag = (1 - core) * 2 + (1 - x_lo)

    def of_local(z_new, e_new):
        return ((z_new * 2 + e_new % 2) * 2 + e_new // 2, t)

    dev_yp = (r, x_hi * NY + yp)
    dev_ym = (r, x_hi * NY + ym)
    ways = (dev_yp, dev_ym)
    t_far = (1 - x_hi) * NY + y
    dev_far = (r, t_far)

    names = {}
    pending = []

    def index_of(name):
        return names.setdefault(name, len(names))

    def send(name, src, dst, device):
        i = index_of(name)
        copy = pltpu.make_async_remote_copy(
            src_ref=src,
            dst_ref=dst,
            send_sem=ssem.at[i],
            recv_sem=rsem.at[i],
            device_id=device,
            device_id_type=MESH,
        )
        copy.start()
        pending.append(copy)

    def arrive(name, landing):
        i = index_of(name)
        pltpu.make_async_remote_copy(
            src_ref=landing,
            dst_ref=landing,
            send_sem=ssem.at[i],
            recv_sem=rsem.at[i],
            device_id=dev_yp,
            device_id_type=MESH,
        ).wait_recv()

    local = {}

    def fetch(name, src, dst):
        i = len(local)
        copy = pltpu.make_async_copy(src, dst, lsem.at[i])
        copy.start()
        local[name] = copy

    blocks = tokens_n // LANES
    fblocks = feats // LANES
    share = delta.shape[1] // (LOCAL * zs)
    frag = delta.shape[0]
    width = share // LANES
    t_ym, t_yp, t_y2 = x_hi * NY + ym, x_hi * NY + yp, x_hi * NY + y2
    f_ym, f_yp, f_y2 = ((1 - x_hi) * NY + k for k in (ym, yp, y2))

    def rows_of(b):
        return pl.ds(pl.multiple_of(b * LANES, LANES), LANES)

    def lane_sum_row(acc):
        return jnp.sum(acc.T, axis=0, keepdims=True)

    def column_of(row):
        return jnp.broadcast_to(row, (LANES, LANES)).T

    def load():
        fetch("delta", delta_hbm, delta)
        fetch("gain", gain_hbm, gain)
        for h in range(2):
            fetch(("tok", h), tok_hbm.at[H[h]], tok.at[H[h]])
        fetch("weight", weight_hbm, wt)
        fetch("cot", cot_hbm, cotg.at[t])

    far_first = sorted(range(1, zs), key=lambda d: -min(d, zs - d))

    def tell(device):
        pl.semaphore_signal(
            pltpu.get_barrier_semaphore(), inc=1, device_id=device, device_id_type=MESH
        )

    def greet():
        for d in range(1, GROUP):
            tell((r - core, (t + d) % GROUP))
        tell(of_local(z, 1 - x_lo))

        @pl.when(core == 1)
        def _():
            tell(of_local(z, x_lo))

    def greet_z():
        for d in far_first:
            tell(of_local((z + d) % zs, 2))
            tell(of_local((z + d) % zs, 3))

    def collect(collector, count, ready_sem):
        @pl.when(core == collector)
        def _():
            pl.semaphore_wait(pltpu.get_barrier_semaphore(), count)
            pl.semaphore_signal(
                ready_sem, inc=1, device_id=of_local(z, e_core), device_id_type=MESH
            )

        @pl.when(core != collector)
        def _():
            pl.semaphore_wait(ready_sem, 1)

    def meet():
        collect(0, 2 * GROUP + 1, ready.at[0])

    def meet_z():
        collect(1, LOCAL * (zs - 1), ready.at[1])

    def cot_start(i):
        h, k = H[i], H[1 - i]
        send(("own_p", i), cot_hbm.at[h], cotg.at[t, h], dev_yp)
        send(("own_m", 1 - i), cot_hbm.at[k], cotg.at[t, k], dev_ym)
        send(("c", i), cot_hbm.at[h], cotg.at[t, h], dev_far)

    def cot_onward(way):
        block = (t_ym, t_yp)[way]
        arrive((("own_p", "own_m")[way], way), cotg.at[block, H[way]])
        send(("own_on", way), cotg.at[block, H[way]], cotg.at[block, H[way]], ways[way])

    def cot_far_start(h):
        arrive(("c", h), cotg.at[t_far, H[h]])
        send(("far_p", h), cotg.at[t_far, H[h]], cotg.at[t_far, H[h]], dev_yp)
        send(("far_m", h), cotg.at[t_far, H[h]], cotg.at[t_far, H[h]], dev_ym)

    def cot_far_onward(way):
        block = (f_ym, f_yp)[way]
        arrive((("far_p", "far_m")[way], way), cotg.at[block, H[way]])
        send(("far_on", way), cotg.at[block, H[way]], cotg.at[block, H[way]], ways[way])

    def cot_own_end():
        local["cot"].wait()
        arrive(("own_p", 1), cotg.at[t_ym, H[1]])
        arrive(("own_m", 0), cotg.at[t_yp, H[0]])
        arrive(("own_on", 0), cotg.at[t_y2, H[0]])
        arrive(("own_on", 1), cotg.at[t_y2, H[1]])

    def cot_far_end():
        arrive(("far_m", 0), cotg.at[f_yp, H[0]])
        arrive(("far_p", 1), cotg.at[f_ym, H[1]])
        arrive(("far_on", 0), cotg.at[f_y2, H[0]])
        arrive(("far_on", 1), cotg.at[f_y2, H[1]])

    def sum_squares():
        def one(b):
            rows = rows_of(b)
            acc = jnp.zeros((LANES, LANES), F32)
            for j in range(fblocks):
                cols = slice(j * LANES, (j + 1) * LANES)
                v = tok[rows, cols].astype(F32)
                acc = acc + v * v
                scaled[rows, cols] = (v * gain[:, cols]).astype(BF16)
            sums[t, pl.ds(b, 1), :] = lane_sum_row(acc)

        local["gain"].wait()
        for h in range(2):
            local[("tok", h)].wait()
            pl.loop(h * blocks // 2, (h + 1) * blocks // 2)(one)

    def sum_squares_send():
        for d in range(1, GROUP):
            send(("sum", d), sums.at[t], sums.at[t], (r, (t + d) % GROUP))

    def sum_squares_end():
        for d in range(1, GROUP):
            arrive(("sum", d), sums.at[(t + GROUP - d) % GROUP])
        total = sums[0]
        for k in range(1, GROUP):
            total = total + sums[k]
        inv_row[...] = lax.rsqrt(total / full_width + EPSILON)

    def normed_rows(first, last):
        @pl.loop(first * blocks // 2, last * blocks // 2)
        def _(b):
            rows = rows_of(b)
            column = column_of(inv_row[pl.ds(b, 1), :])
            inv_col[rows, :] = column
            for j in range(fblocks):
                cols = slice(j * LANES, (j + 1) * LANES)
                value = (tok[rows, cols].astype(F32) * column * gain[:, cols]).astype(BF16)
                normed_t[cols, rows] = value.T

    def weight_ready():
        local["weight"].wait()

    def key_parts(x_side):
        @pl.loop(0, 2)
        def _(k):
            n = x_side * 2 + k
            cols = pl.ds(pl.multiple_of(n * 2 * LANES, LANES), 2 * LANES)
            for h in range(2):
                part = jnp.dot(scaled[H[h], :], wt[:, cols], preferred_element_type=F32)
                parts[2 * n, H[h]] = part[:, :LANES].astype(BF16)
                parts[2 * n + 1, H[h]] = part[:, LANES:].astype(BF16)

    def own_at(y_new):
        return x_hi * NY + y_new

    def far_at(y_new):
        return (1 - x_hi) * NY + y_new

    def plus(first, second):
        return (first.astype(F32) + second.astype(F32)).astype(BF16)

    def key_far_start(role):
        plus_block, minus_block = ((ym, yp), (yp, ym))[role]
        send(("g_p", role), parts.at[far_at(plus_block), H[1]], gin.at[role, 1], dev_yp)
        send(("g_m", role), parts.at[far_at(minus_block), H[0]], gin.at[role, 0], dev_ym)

    def key_cross(role, h):
        block = far_at((y2, y)[role])
        arrive((("g_m", "g_p")[h], role), gin.at[role, h])
        xout[role, h] = plus(gin[role, h], parts[block, H[h]])
        send(("x", role, h), xout.at[role, h], cin.at[role, h], dev_far)

    def key_own_start():
        send("d1p", parts.at[own_at(yp), H[1]], near.at[0, H[1]], dev_yp)
        send("d1m", parts.at[own_at(ym), H[0]], near.at[1, H[0]], dev_ym)

    def key_two_away(way):
        arrive(("x", 0, way), cin.at[0, way])
        two_out[way] = plus(cin[0, way], parts[own_at(y2), H[way]])
        send(("d2", way), two_out.at[way], merge_in.at[way], ways[way])

    def key_merge(way):
        arrive(("d2", way), merge_in.at[way])
        merge_out[way] = plus(merge_in[way], parts[own_at((yp, ym)[way]), H[way]])
        send(("d1", way), merge_out.at[way], near.at[way, H[way]], ways[way])

    def key_end():
        arrive("d1p", near.at[0, H[1]])
        arrive("d1m", near.at[1, H[0]])
        for h in range(2):
            arrive(("x", 1, h), cin.at[1, h])
        for h in range(2):
            arrive(("d1", h), near.at[h, H[h]])
            total = parts[own_at(y), H[h]].astype(F32) + cin[1, h].astype(F32)
            total = total + (near[0, H[h]].astype(F32) + near[1, H[h]].astype(F32))
            keys_ref[H[h], :] = (total * inv_col[H[h], :]).astype(BF16)

    def weight_grad(first, last):
        @pl.loop(first, last)
        def _(k):
            weight_grad_pair(x_hi * 2 + k, cotg, normed_t, wgrad_ref)

    def project(x_side):
        @pl.loop(0, blocks)
        def _(b):
            rows = rows_of(b)
            acc = jnp.zeros((LANES, LANES), F32)
            for k in range(NY):
                block = x_side * NY + k
                acc = acc + cotg[block, rows, :].astype(F32) * parts[block, rows, :].astype(F32)
            half_proj[x_side, pl.ds(b, 1), :] = lane_sum_row(acc)

    step = 2 * LANES
    steps = tokens_n // step

    def cot_times_weight(x_side, rows):
        lhs = jnp.concatenate([cotg[x_side * NY + k, rows, :] for k in range(NY)], axis=1)
        cols = pl.ds(pl.multiple_of(x_side * NY * LANES, LANES), NY * LANES)
        return lax.dot_general(
            lhs, wt[:, cols], (((1,), (1,)), ((), ())), preferred_element_type=F32
        )

    def normed_grads_own(first, last):
        @pl.loop(first * steps // 4, last * steps // 4)
        def _(m):
            rows = pl.ds(pl.multiple_of(m * step, step), step)
            dpart[rows, :] = cot_times_weight(x_hi, rows)

    def proj_send():
        projs[t] = half_proj[0] + half_proj[1]
        for d in range(1, GROUP):
            send(("proj", d), projs.at[t], projs.at[t], (r, (t + d) % GROUP))

    def proj_end():
        for d in range(1, GROUP):
            arrive(("proj", d), projs.at[(t + GROUP - d) % GROUP])
        total = projs[0]
        for k in range(1, GROUP):
            total = total + projs[k]
        projected = total * inv_row[...] / full_width
        rowproj_ref[...] = projected * math.sqrt(full_width)
        other_row[...] = projected * inv_row[...] * inv_row[...]

    def token_grads(first, last):
        @pl.loop(first * steps // 4, last * steps // 4)
        def _(m):
            rows = pl.ds(pl.multiple_of(m * step, step), step)
            d = dpart[rows, :] + cot_times_weight(1 - x_hi, rows)
            column = inv_col[rows, :]
            other = jnp.concatenate(
                [column_of(other_row[pl.ds(2 * m + k, 1), :]) for k in range(2)], axis=0
            )
            for j in range(fblocks):
                cols = slice(j * LANES, (j + 1) * LANES)
                tgrad_ref[rows, cols] = (
                    column * (d[:, cols] * gain[:, cols]) - tok[rows, cols].astype(F32) * other
                ).astype(BF16)

    def quantize(first, last):
        if first == 0:
            local["delta"].wait()
        ones_blocks = block_ones()

        @pl.loop(first * zs // 2, last * zs // 2)
        def _(i):
            shares = (2 * i, 2 * i + 1)
            pieces = [
                delta[:, pl.ds(pl.multiple_of(s * share + k * LANES, LANES), LANES)]
                for s in shares
                for k in range(width)
            ]
            values = jnp.concatenate([v.astype(F32) for v in pieces], axis=0).astype(BF16)
            coded = quantized(values, ones_blocks)
            for n, s in enumerate(shares):
                qsend[s % LOCAL, s // LOCAL] = coded[n * width * frag : (n + 1) * width * frag]

    share_rows = qsend.shape[2]
    cut = share_rows // 32 * 16
    pieces = (slice(0, share_rows - cut), slice(share_rows - cut, share_rows))

    def delta_start(i):
        p = pieces[i]
        for d in (2, 1, 3):
            to = (e + d) % LOCAL
            send(("r1", i, d), qsend.at[to, :, p], r1.at[e, :, p], of_local(z, to))

    def delta_sum(i):
        p = pieces[i]
        r1[e, :, p, :] = qsend[e, :, p, :]
        for d in range(1, LOCAL):
            arrive(("r1", i, d), r1.at[(e + LOCAL - d) % LOCAL, :, p])

        @pl.loop(0, zs)
        def _(k):
            s1[k, p, :] = (r1[0, k, p, :].astype(F32) + r1[1, k, p, :].astype(F32)) + (
                r1[2, k, p, :].astype(F32) + r1[3, k, p, :].astype(F32)
            )

        r2[z, p, :] = s1[z, p, :]

    def delta_z(i):
        p = pieces[i]
        for d in far_first:
            to = (z + d) % zs
            send(("r2", i, d), s1.at[to, p], r2.at[z, p], of_local(to, e))

    def delta_average(i):
        p = pieces[i]
        for d in range(1, zs):
            arrive(("r2", i, d), r2.at[(z + zs - d) % zs, p])
        total = r2[0, p, :]
        for k in range(1, zs):
            total = total + r2[k, p, :]
        upd[e, z, p, :] = quantized(total / (LOCAL * zs), block_ones()).astype(BF16)
        mine = upd.at[e, z, p]
        for d in (*far_first, 0):
            send(("r3x", i, d), mine, mine, of_local((z + d) % zs, e_xlo))
        for d in far_first:
            send(("r3", i, d), mine, mine, of_local((z + d) % zs, e))

    def update_core(i):
        p = pieces[i]
        for d in range(zs):
            arrive(("r3x", i, d), upd.at[e_xlo, (z + zs - d) % zs, p])
        for d in range(1, zs):
            arrive(("r3", i, d), upd.at[e, (z + zs - d) % zs, p])
        both = upd.at[pl.ds(core * 2, 2), :, p]
        send(("r4", i), both, both, of_local(z, e_core))

    def update_end():
        for i, p in enumerate(pieces):
            arrive(("r4", i), upd.at[pl.ds((1 - core) * 2, 2), :, p])

    greet()
    load()
    meet()
    cot_start(0)
    greet_z()
    cot_start(1)
    quantize(0, 4)
    delta_start(0)
    delta_start(1)
    sum_squares()
    weight_ready()
    key_parts(1 - x_hi)
    key_far_start(0)
    sum_squares_send()
    cot_onward(0)
    cot_onward(1)
    cot_far_start(0)
    key_parts(x_hi)
    delta_sum(0)
    meet_z()
    delta_z(0)
    key_cross(0, 0)
    key_cross(0, 1)
    cot_far_start(1)
    key_far_start(1)
    delta_sum(1)
    delta_z(1)
    sum_squares_end()
    normed_rows(0, 2)
    key_two_away(0)
    key_two_away(1)
    cot_own_end()
    project(x_hi)
    cot_far_onward(0)
    cot_far_onward(1)
    delta_average(0)
    key_own_start()
    key_cross(1, 0)
    key_cross(1, 1)
    delta_average(1)
    key_merge(0)
    key_merge(1)
    weight_grad(0, 1)
    cot_far_end()
    project(1 - x_hi)
    proj_send()
    weight_grad(1, 2)
    normed_grads_own(0, 2)
    update_core(0)
    normed_grads_own(2, 4)
    proj_end()
    token_grads(0, 1)
    update_core(1)
    token_grads(1, 4)
    key_end()
    update_end()

    for copy in pending:
        copy.wait_send()


def finish_kernel(
    keys_ref,
    tgrad_ref,
    rowproj_ref,
    wgrad_ref,
    upd_ref,
    cotg_ref,
    normed_t_ref,
    params_ref,
    momentum_ref,
    keys_hbm,
    tgrad_hbm,
    rowproj_hbm,
    wgrad_hbm,
    params_hbm,
    momentum_hbm,
    wgrad_far,
    new_params,
    new_momentum,
    sem,
):
    x_hi = lax.axis_index("tensor") // NY
    heads = wgrad_ref.shape[1]
    own = pl.ds(pl.multiple_of(x_hi * (heads // 2), LANES), heads // 2)
    copies = []

    def write(src, dst):
        copy = pltpu.make_async_copy(src, dst, sem.at[len(copies)])
        copy.start()
        copies.append(copy)

    write(tgrad_ref, tgrad_hbm)
    write(wgrad_ref.at[:, own], wgrad_hbm.at[:, own])
    write(keys_ref, keys_hbm)
    write(rowproj_ref, rowproj_hbm)

    rows, columns = new_params.shape
    zs = upd_ref.shape[1]
    share = columns // (LOCAL * zs)
    groups = 4 if zs % 4 == 0 else 1
    for g in range(groups):

        @pl.loop(g * LOCAL * zs // groups, (g + 1) * LOCAL * zs // groups)
        def _(s):
            update = upd_ref[s % LOCAL, s // LOCAL].astype(F32)
            for k in range(share // LANES):
                cols = pl.ds(pl.multiple_of(s * share + k * LANES, LANES), LANES)
                piece = update[k * rows : (k + 1) * rows, :]
                moved = OUTER_MOMENTUM * momentum_ref[:, cols] + piece
                new_momentum[:, cols] = moved
                new_params[:, cols] = params_ref[:, cols] - OUTER_RATE * (
                    piece + OUTER_MOMENTUM * moved
                )

        cols = pl.ds(g * (columns // groups), columns // groups)
        write(new_params.at[:, cols], params_hbm.at[:, cols])
        write(new_momentum.at[:, cols], momentum_hbm.at[:, cols])

    for k in range(2):
        pair = (1 - x_hi) * 2 + k
        weight_grad_pair(pair, cotg_ref, normed_t_ref, wgrad_far)
        cols = pl.ds(pl.multiple_of(pair * 2 * LANES, LANES), 2 * LANES)
        write(wgrad_far.at[:, cols], wgrad_hbm.at[:, cols])
    for copy in copies:
        copy.wait()


def per_device(tokens, norm_gain, key_weight, key_cotangent, local_delta, outer_params, momentum):
    tok_n, feats = tokens.shape
    heads = key_weight.shape[1]
    full_width = feats * lax.axis_size("tensor")
    workers = lax.axis_size("replica")
    zs = workers // LOCAL
    frag, row_width = outer_params.shape
    share_rows = frag * row_width // workers // LANES
    half = tok_n // 2
    kb = key_cotangent.shape[1]
    hbm = pl.BlockSpec(memory_space=pltpu.HBM)
    vmem = pl.BlockSpec(memory_space=pltpu.VMEM)
    blocks = tok_n // LANES
    operands = (tokens, norm_gain.reshape(1, feats), key_weight, key_cotangent, local_delta[0])
    results = pl.pallas_call(
        functools.partial(kernel, full_width),
        out_shape=(
            jax.ShapeDtypeStruct((tok_n, kb), BF16),
            jax.ShapeDtypeStruct((tok_n, feats), BF16),
            jax.ShapeDtypeStruct((blocks, LANES), F32),
            jax.ShapeDtypeStruct((feats, heads), BF16),
            jax.ShapeDtypeStruct((LOCAL, zs, share_rows, LANES), BF16),
            jax.ShapeDtypeStruct((GROUP, tok_n, kb), BF16),
            jax.ShapeDtypeStruct((feats, tok_n), BF16),
        ),
        in_specs=[hbm] * 5,
        out_specs=(vmem,) * 7,
        scratch_shapes=[
            pltpu.VMEM((tok_n, feats), BF16),
            pltpu.VMEM((1, feats), F32),
            pltpu.VMEM(local_delta.shape[1:], BF16),
            pltpu.VMEM((feats, heads), BF16),
            pltpu.VMEM((tok_n, feats), BF16),
            pltpu.VMEM((GROUP, tok_n, kb), BF16),
            pltpu.VMEM((tok_n, feats), F32),
            pltpu.VMEM((tok_n, LANES), F32),
            pltpu.VMEM((blocks, LANES), F32),
            pltpu.VMEM((blocks, LANES), F32),
            pltpu.VMEM((GROUP, blocks, LANES), F32),
            pltpu.VMEM((GROUP, blocks, LANES), F32),
            pltpu.VMEM((2, blocks, LANES), F32),
            pltpu.VMEM((2, 2, half, kb), BF16),
            pltpu.VMEM((2, 2, half, kb), BF16),
            pltpu.VMEM((2, 2, half, kb), BF16),
            pltpu.VMEM((2, half, kb), BF16),
            pltpu.VMEM((2, half, kb), BF16),
            pltpu.VMEM((2, half, kb), BF16),
            pltpu.VMEM((2, tok_n, kb), BF16),
            pltpu.VMEM((LOCAL, zs, share_rows, LANES), BF16),
            pltpu.VMEM((LOCAL, zs, share_rows, LANES), BF16),
            pltpu.VMEM((zs, share_rows, LANES), F32),
            pltpu.VMEM((zs, share_rows, LANES), F32),
            pltpu.SemaphoreType.REGULAR((2,)),
            pltpu.SemaphoreType.DMA((N_REMOTE,)),
            pltpu.SemaphoreType.DMA((N_REMOTE,)),
            pltpu.SemaphoreType.DMA((N_LOCAL,)),
        ],
        compiler_params=pltpu.CompilerParams(
            collective_id=0, has_side_effects=True, vmem_limit_bytes=36 * 1024 * 1024
        ),
        cost_estimate=pl.CostEstimate(
            flops=6 * tok_n * feats * heads, bytes_accessed=16 * 1024 * 1024, transcendentals=0
        ),
    )(*(pltpu.with_memory_space_constraint(a, pltpu.HBM) for a in operands))
    keys, tgrad, rowproj, wgrad, new_params, new_momentum = pl.pallas_call(
        finish_kernel,
        out_shape=(
            jax.ShapeDtypeStruct((tok_n, kb), BF16),
            jax.ShapeDtypeStruct((tok_n, feats), BF16),
            jax.ShapeDtypeStruct((blocks, LANES), F32),
            jax.ShapeDtypeStruct((feats, heads), BF16),
            jax.ShapeDtypeStruct((frag, row_width), F32),
            jax.ShapeDtypeStruct((frag, row_width), F32),
        ),
        in_specs=[vmem] * 9,
        out_specs=(hbm,) * 6,
        scratch_shapes=[
            pltpu.VMEM((feats, heads), BF16),
            pltpu.VMEM((frag, row_width), F32),
            pltpu.VMEM((frag, row_width), F32),
            pltpu.SemaphoreType.DMA((16,)),
        ],
        compiler_params=pltpu.CompilerParams(vmem_limit_bytes=16 * 1024 * 1024),
        cost_estimate=pl.CostEstimate(
            flops=8 * frag * row_width, bytes_accessed=8 * 1024 * 1024, transcendentals=0
        ),
    )(*results, outer_params, momentum)
    return (keys, tgrad, rowproj.reshape(tok_n), wgrad[None], new_params, new_momentum)


def solution(mesh):
    placed = (
        P("replica", "tensor"),
        P("tensor"),
        P("tensor", None),
        P("replica", "tensor"),
        P("replica", "tensor", None),
        P("tensor", None),
        P("tensor", None),
    )
    return jax.shard_map(
        per_device,
        mesh=mesh,
        in_specs=placed,
        out_specs=(
            P("replica", "tensor"),
            P("replica", "tensor"),
            P("replica"),
            P("replica", "tensor", None),
            P("tensor", None),
            P("tensor", None),
        ),
        check_vma=False,
    )
```
